32 devices in a mesh: row: 4 (over y, x), col: 8 (over z, core).
Axes of the slice: x: 2, y: 2, z: 4, core: 2. Of those that a mesh axis runs over, the one named last changes fastest.
Arguments:
- start_block: float32 [32, 12288], P(None, ('row', 'col')), may hold values from -6 to 6
- center: float32 [1], replicated, may hold values from 1.05 to 1.15
- half_width: float32 [1], replicated, may hold values from 0.85 to 0.95
- matrix_tiles: bfloat16 [4, 384, 192, 192], P('row', 'col')
- tile_row: int32 [4, 384], P('row', 'col'), may hold values from 0 to 15, as said below
- tile_col: int32 [4, 384], P('row', 'col'), may hold values from 0 to 7, as said below
- tile_live: int32 [4, 384], P('row', 'col'), may hold values from 0 to 1
Outputs:
- filtered: float32 [32, 12288], P(None, ('row', 'col'))
- previous: float32 [32, 12288], P(None, ('row', 'col'))
The draws below stay inside these ranges and needn't reach their ends.
Inputs may be any that keep to these rules, and one draw needn't show every extreme that they name: tile_row lies within the device's row clusters; on a live slot the block row's atom order is at most the block column's. tile_col lies within the device's column clusters.
All inputs are finite; a program needn't handle non-finite values.
Results may differ from the reference program's by a relative error of at most 0.03.
Values may be sent and summed in bfloat16 or wider, within the bound.
A program may use at most 64 MiB of HBM per device.

```python
import math
import jax
import jax.numpy as jnp
from jax import lax

B = 192
K = 32
DEG = 8
CL_DEV = 2
SLOTS = 48
NC = 64
N = 12288
N_ROW = 4
N_COL = 8


def pattern(key):
    panel_cols = CL_DEV * N_ROW
    factor = N_COL // N_ROW
    band_reach = max(2, SLOTS // (CL_DEV * N_COL))
    shape_all = (N_ROW, N_COL * SLOTS)
    row_grid = jnp.broadcast_to(jnp.arange(N_ROW, dtype=jnp.int32)[:, None], shape_all)
    flat_slot = jnp.broadcast_to(jnp.arange(N_COL * SLOTS, dtype=jnp.int32)[None, :], shape_all)
    col_grid = flat_slot // SLOTS
    slot_index = flat_slot % SLOTS
    base = jax.random.fold_in(key, 11)
    key_col, key_sub, key_step, key_live = jax.random.split(base, 4)
    col_local = jax.random.randint(key_col, shape_all, 0, panel_cols, dtype=jnp.int32)
    sub_row = jax.random.randint(key_sub, shape_all, 0, factor, dtype=jnp.int32)
    step_back = jax.random.randint(key_step, shape_all, 0, band_reach, dtype=jnp.int32)
    coin = jax.random.randint(key_live, shape_all, 0, 4, dtype=jnp.int32)
    row_block = row_grid * factor + sub_row
    row_local = col_local - step_back
    broken = (row_local < 0) | (step_back == 0) & (row_block > col_grid)
    diagonal = (col_grid // factor == row_grid) & (slot_index < panel_cols)
    col_local = jnp.where(diagonal, slot_index, col_local)
    sub_row = jnp.where(diagonal, col_grid - row_grid * factor, sub_row)
    row_local = jnp.where(diagonal, slot_index, jnp.clip(row_local, 0, panel_cols - 1))
    live = jnp.where(diagonal | ~broken & (coin > 0), 1, 0).astype(jnp.int32)
    row_ids = (sub_row * panel_cols + row_local).astype(jnp.int32)
    return (row_ids, col_local.astype(jnp.int32), live, diagonal)


def draw_tile_row(key, part):
    shared = pattern(key)
    return shared[0]


def draw_tile_col(key, part):
    shared = pattern(key)
    return shared[1]


def draw_tile_live(key, part):
    shared = pattern(key)
    return shared[2]


def draw_matrix_tiles(key, part):
    shared = pattern(key)
    key = jax.random.fold_in(key, 5)
    scale = 0.45 / math.sqrt(1.2 * SLOTS * B / CL_DEV)
    shape_all = (N_ROW, N_COL * SLOTS, B, B)
    noise = jax.random.normal(key, shape_all, jnp.float32) * scale
    identity = jnp.eye(B, dtype=jnp.float32)
    shift = shared[3].astype(jnp.float32)[:, :, None, None] * 0.5 * identity[None, None, :, :]
    return (noise + shift).astype(jnp.bfloat16)


def level_of(key, extent, cuts, smallest, top_value):
    level, own = 1.0, jax.random.fold_in(key, 6)
    for dim, parts in cuts:
        heights = jnp.exp(jax.random.uniform(jax.random.fold_in(own, dim), (parts,), jnp.float32, smallest / len(cuts), top_value / len(cuts)))
        level = level * jnp.repeat(heights, extent[dim] // parts).reshape([-1 if axis == dim else 1 for axis in range(len(extent))])
    return level


def gaussian(key, extent, scale, limit, cuts=(), kind=jnp.bfloat16):
    drawn = scale * jax.random.normal(key, extent, jnp.float32)
    if cuts:
        drawn = drawn * level_of(key, extent, cuts, -0.22, 0.18)
    return jnp.clip(drawn, -limit, limit).astype(kind)


def setup_inputs(seed: int = 0) -> dict:
    splits = jax.random.split(jax.random.key(seed), 8)
    start_block = gaussian(splits[0], (K, N), 1.0, 6.0, ((1, 32),), jnp.float32)
    center = jnp.clip(jax.random.uniform(splits[1], (1,), jnp.float32, 1.05, 1.15), 1.05, 1.15)
    half_width = jnp.clip(jax.random.uniform(splits[2], (1,), jnp.float32, 0.85, 0.95), 0.85, 0.95)
    matrix_tiles = draw_matrix_tiles(jax.random.fold_in(splits[7], 71), 0)
    tile_row = draw_tile_row(jax.random.fold_in(splits[7], 71), 0)
    tile_col = draw_tile_col(jax.random.fold_in(splits[7], 71), 0)
    tile_live = draw_tile_live(jax.random.fold_in(splits[7], 71), 0)
    return {"start_block": start_block, "center": center, "half_width": half_width, "matrix_tiles": matrix_tiles, "tile_row": tile_row, "tile_col": tile_col, "tile_live": tile_live}


def apply_matrix(row_vectors, matrix_tiles, tile_row, tile_col, tile_live):
    panel_rows = CL_DEV * N_COL
    panel_cols = CL_DEV * N_ROW
    zero_index = jnp.zeros((), jnp.int32)

    def visit(totals, device):
        row_index = (device // N_COL).astype(jnp.int32)
        col_index = (device % N_COL).astype(jnp.int32)
        slot_start = (col_index * SLOTS).astype(jnp.int32)
        stored = lax.dynamic_slice(matrix_tiles, (row_index, slot_start, zero_index, zero_index), (1, SLOTS, B, B))[0].astype(jnp.float32)
        row_ids = lax.dynamic_slice(tile_row, (row_index, slot_start), (1, SLOTS))[0] + row_index * panel_rows
        col_ids = lax.dynamic_slice(tile_col, (row_index, slot_start), (1, SLOTS))[0] + col_index * panel_cols
        weights = lax.dynamic_slice(tile_live, (row_index, slot_start), (1, SLOTS))[0].astype(jnp.float32)
        row_ids = row_ids.astype(jnp.int32)
        col_ids = col_ids.astype(jnp.int32)
        x_col = row_vectors[:, col_ids, :]
        x_row = row_vectors[:, row_ids, :]
        direct = jnp.einsum("ksb,sab->ksa", x_col, stored, precision=lax.Precision.HIGHEST) * weights[None, :, None]
        mirrored = jnp.einsum("ksa,sab->ksb", x_row, stored, precision=lax.Precision.HIGHEST) * weights[None, :, None]
        totals = totals.at[:, row_ids, :].add(direct)
        totals = totals.at[:, col_ids, :].add(mirrored)
        return totals, None

    start = jnp.zeros(row_vectors.shape, jnp.float32)
    totals, _ = lax.scan(visit, start, jnp.arange(N_ROW * N_COL, dtype=jnp.int32))
    return totals


def advance(degree, product, current, earlier, center_value, half_value):
    if degree == 0:
        return (product - center_value * current) / half_value
    return 2.0 * (product - center_value * current) / half_value - earlier


def reference(start_block, center, half_width, matrix_tiles, tile_row, tile_col, tile_live):
    current = start_block.reshape(K, NC, B)
    earlier = current
    for degree in range(DEG):
        rounded = current.astype(jnp.bfloat16).astype(jnp.float32)
        product = apply_matrix(rounded, matrix_tiles, tile_row, tile_col, tile_live)
        following = advance(degree, product, current, earlier, center[0], half_width[0])
        earlier, current = current, following
    return current.reshape(K, N), earlier.reshape(K, N)
```

```python
import functools

import jax
import jax.numpy as jnp
from jax import lax
from jax.experimental import pallas as pl
from jax.experimental.pallas import tpu as pltpu
from jax.sharding import PartitionSpec as P

DEG = 8
MESH = pl.DeviceIdType.MESH
BF = jnp.bfloat16
F32 = jnp.float32


def build_kernel(slots, panel_cols, tile, rows_ref, cols_ref, live_ref, tiles_ref, out_ref, head, link, acc):
    block_row = pl.program_id(0)

    @pl.when(block_row == 0)
    def _():
        @pl.loop(0, pl.num_programs(0) * panel_cols)
        def _(b):
            head[b] = -1

        @pl.loop(0, slots)
        def _(s):
            @pl.when(live_ref[s] > 0)
            def _():
                b = rows_ref[s] * panel_cols + cols_ref[s]
                link[s] = head[b]
                head[b] = s

    for pair in range(panel_cols // 2):
        for side in range(2):
            s = head[block_row * panel_cols + 2 * pair + side]

            @pl.when(s < 0)
            def _(side=side):
                acc[side] = jnp.zeros((tile, tile), F32)

            @pl.when(s >= 0)
            def _(side=side, s=s):
                acc[side] = tiles_ref[s].astype(F32)

                def more(t):
                    acc[side] += tiles_ref[t].astype(F32)
                    return link[t]

                lax.while_loop(lambda t: t >= 0, more, link[s])

        both = jnp.concatenate([acc[0], acc[1]], axis=1)
        out_ref[:, pair * 2 * tile : (pair + 1) * 2 * tile] = both.astype(BF)


def build_panel(tiles, row_ids, col_ids, live, panel_rows, panel_cols):
    slots, tile, _ = tiles.shape
    smem = pl.BlockSpec(memory_space=pltpu.SMEM)
    return pl.pallas_call(
        functools.partial(build_kernel, slots, panel_cols, tile),
        grid=(panel_rows,),
        out_shape=jax.ShapeDtypeStruct((panel_rows * tile, panel_cols * tile), BF),
        in_specs=[smem, smem, smem, pl.BlockSpec((slots, tile, tile), lambda i: (0, 0, 0))],
        out_specs=pl.BlockSpec((tile, panel_cols * tile), lambda i: (i, 0)),
        scratch_shapes=[
            pltpu.SMEM((panel_rows * panel_cols,), jnp.int32),
            pltpu.SMEM((slots,), jnp.int32),
            pltpu.VMEM((2, tile, tile), F32),
        ],
        compiler_params=pltpu.CompilerParams(vmem_limit_bytes=32 * 2**20),
    )(row_ids, col_ids, live, tiles)


def filter_kernel(
    R, C, panel_ref, start_ref, center_ref, half_ref, out_ref, prev_ref,
    rowp, colp, sendr, sendc, redr, redc, mir, own,
    ps_row, ps_col, pr_row, pr_col, rs_row, rs_col, rr_row, rr_col,
):
    w = start_ref.shape[1]
    w2 = 2 * w
    Z = C // 2
    r = lax.axis_index("row")
    c = lax.axis_index("col")
    z, core = c // 2, c % 2
    root_row = c * R // C
    off = c * R % C
    is_root = r == root_row
    not_root = r != root_row
    col_home = (r * C + c) // R
    col_slot = c % R

    def col_of(d):
        return (c + d) % C

    def row_of(d):
        return (r + d) % R

    def chunk(d):
        return 2 * ((z // 2 + d // 2) % (Z // 2)) + (z % 2 + d % 2) % 2

    def remote(src, dst, send_sem, recv_sem, row, col):
        return pltpu.make_async_remote_copy(
            src_ref=src, dst_ref=dst, send_sem=send_sem, recv_sem=recv_sem,
            device_id=(row, col), device_id_type=MESH,
        )

    barrier = pltpu.get_barrier_semaphore()
    for d in range(1, C):
        pl.semaphore_signal(barrier, inc=1, device_id=(r, col_of(d)), device_id_type=MESH)
    for d in range(1, R):
        pl.semaphore_signal(barrier, inc=1, device_id=(row_of(d), col_home), device_id_type=MESH)

    @pl.when(not_root)
    def _():
        for i in range(R):
            pl.semaphore_signal(barrier, inc=1, device_id=(root_row, off + i), device_id_type=MESH)

    pl.semaphore_wait(barrier, jnp.where(is_root, C + R - 2, C + 2 * R - 2))

    out_ref[...] = start_ref[...]
    prev_ref[...] = start_ref[...]

    def p_row(par, d):
        return remote(rowp.at[par, c], rowp.at[par, c], ps_row.at[d], pr_row.at[par, c], r, col_of(d))

    def p_row_in(par, src):
        return remote(rowp.at[par, src], rowp.at[par, src], ps_row.at[0], pr_row.at[par, src], r, src)

    def p_col(par, d):
        return remote(rowp.at[par, c], colp.at[par, col_slot], ps_col.at[d], pr_col.at[par, col_slot], row_of(d), col_home)

    def p_col_in(par, i):
        return remote(colp.at[par, i], colp.at[par, i], ps_col.at[0], pr_col.at[par, i], root_row, off + i)

    def s_row(par, dst):
        return remote(sendr.at[dst], redr.at[par, c], rs_row.at[dst], rr_row.at[par, c], r, dst)

    def s_row_in(par, src):
        return remote(redr.at[par, src], redr.at[par, src], rs_row.at[src], rr_row.at[par, src], r, src)

    def s_col(par, i):
        return remote(sendc.at[i], redc.at[par, r], rs_col.at[i], rr_col.at[par, r], root_row, off + i)

    def s_col_in(par, src):
        return remote(redc.at[par, src], redc.at[par, src], rs_col.at[0], rr_col.at[par, src], src, col_home)

    def wait_sums_sent(par):
        for d in range(1, C):
            s_row(par, col_of(d)).wait_send()

        @pl.when(not_root)
        def _():
            for i in range(R):
                s_col(par, i).wait_send()

    def step(k, carry):
        par = k % 2
        rowp[par, c] = out_ref[...].astype(BF)
        for d in range(1, R):
            p_col(par, d).start()
        for d in range(C - 1, 0, -1):
            p_row(par, d).start()

        @pl.when(k > 0)
        def _():
            wait_sums_sent(1 - par)

        for d in range(Z):
            zz = chunk(d)
            if d == 0:
                p_row_in(par, c + 1 - 2 * core).wait_recv()
            else:
                p_row_in(par, 2 * zz).wait_recv()
                p_row_in(par, 2 * zz + 1).wait_recv()
            lhs = jnp.concatenate([rowp[par, 2 * zz], rowp[par, 2 * zz + 1]], axis=1)
            part = jnp.dot(lhs, panel_ref[pl.ds(zz * w2, w2), :], preferred_element_type=F32)
            for i in range(R // 2):
                piece = part[:, i * w2 : (i + 1) * w2]
                if d == 0:
                    mir[i] = piece
                else:
                    mir[i] += piece

        @pl.when(not_root)
        def _():
            for i in range(R):
                sendc[i] = mir[i // 2, :, (i % 2) * w : (i % 2 + 1) * w].astype(BF)
                s_col(par, i).start()
            for i in range(R):
                p_col_in(par, i).wait_recv()

        @pl.when(is_root)
        def _():
            for i in range(R):
                colp[par, i] = rowp[par, off + i]

        x_col = jnp.concatenate([colp[par, i] for i in range(R)], axis=1)
        for d in range(Z - 1, -1, -1):
            zz = chunk(d)
            part = lax.dot_general(
                x_col, panel_ref[pl.ds(zz * w2, w2), :], (((1,), (1,)), ((), ())),
                preferred_element_type=F32,
            )
            place = zz - off // 2
            inside = is_root & (place >= 0) & (place < R // 2)
            part = part + jnp.where(inside, mir[jnp.clip(place, 0, R // 2 - 1)], 0.0)
            left, right = part[:, :w], part[:, w:]
            sendr[2 * zz] = left.astype(BF)
            sendr[2 * zz + 1] = right.astype(BF)
            if d == 0:
                s_row(par, c + 1 - 2 * core).start()
                own[...] = jnp.where(core == 0, left, right)
            else:
                s_row(par, 2 * zz).start()
                s_row(par, 2 * zz + 1).start()

        total = own[...]
        for d in range(1, R):
            s_col_in(par, row_of(d)).wait_recv()
            total = total + redc[par, row_of(d)].astype(F32)
        for d in range(1, C):
            s_row_in(par, col_of(d)).wait_recv()
            total = total + redr[par, col_of(d)].astype(F32)

        first = k == 0
        scale = jnp.where(first, 1.0, 2.0)
        keep = jnp.where(first, 0.0, 1.0)
        current = out_ref[...]
        following = scale * (total - center_ref[0] * current) / half_ref[0] - keep * prev_ref[...]
        prev_ref[...] = current
        out_ref[...] = following
        for d in range(1, R):
            p_col(par, d).wait_send()
        for d in range(1, C):
            p_row(par, d).wait_send()
        return carry

    lax.fori_loop(0, DEG, step, 0)
    wait_sums_sent((DEG - 1) % 2)


def body(R, C, start_block, center, half_width, matrix_tiles, tile_row, tile_col, tile_live):
    vectors, w = start_block.shape
    tile = matrix_tiles.shape[-1]
    own_clusters = w // tile
    panel = build_panel(
        matrix_tiles[0], tile_row[0], tile_col[0], tile_live[0], own_clusters * C, own_clusters * R
    )
    vmem = pl.BlockSpec(memory_space=pltpu.VMEM)
    smem = pl.BlockSpec(memory_space=pltpu.SMEM)
    dma = pltpu.SemaphoreType.DMA
    flat = jax.ShapeDtypeStruct((vectors, w), F32)
    panel_bytes = panel.shape[0] * panel.shape[1] * 2
    return pl.pallas_call(
        functools.partial(filter_kernel, R, C),
        out_shape=(flat, flat),
        in_specs=[vmem, vmem, smem, smem],
        out_specs=(vmem, vmem),
        scratch_shapes=[
            pltpu.VMEM((2, C, vectors, w), BF),
            pltpu.VMEM((2, R, vectors, w), BF),
            pltpu.VMEM((C, vectors, w), BF),
            pltpu.VMEM((R, vectors, w), BF),
            pltpu.VMEM((2, C, vectors, w), BF),
            pltpu.VMEM((2, R, vectors, w), BF),
            pltpu.VMEM((R // 2, vectors, 2 * w), F32),
            pltpu.VMEM((vectors, w), F32),
            dma((C,)), dma((R,)), dma((2, C)), dma((2, R)),
            dma((C,)), dma((R,)), dma((2, C)), dma((2, R)),
        ],
        compiler_params=pltpu.CompilerParams(
            collective_id=0, has_side_effects=True, vmem_limit_bytes=panel_bytes + 14 * 2**20
        ),
    )(panel, start_block, center, half_width)


def solution(mesh):
    R, C = mesh.shape["row"], mesh.shape["col"]
    in_specs = (
        P(None, ("row", "col")),
        P(),
        P(),
        P("row", "col", None, None),
        P("row", "col"),
        P("row", "col"),
        P("row", "col"),
    )
    out_specs = (P(None, ("row", "col")), P(None, ("row", "col")))
    return jax.shard_map(
        functools.partial(body, R, C), mesh=mesh, in_specs=in_specs, out_specs=out_specs, check_vma=False
    )
```

```python
import functools

import jax
import jax.numpy as jnp
from jax import lax
from jax.experimental import pallas as pl
from jax.experimental.pallas import tpu as pltpu
from jax.sharding import PartitionSpec as P

DEG = 8
MESH = pl.DeviceIdType.MESH
BF = jnp.bfloat16
F32 = jnp.float32


def build_kernel(slots, panel_cols, tile, rows_ref, cols_ref, live_ref, tiles_ref, out_ref, head, link, acc):
    block_row = pl.program_id(0)

    @pl.when(block_row == 0)
    def _():
        @pl.loop(0, pl.num_programs(0) * panel_cols)
        def _(b):
            head[b] = -1

        @pl.loop(0, slots)
        def _(s):
            @pl.when(live_ref[s] > 0)
            def _():
                b = rows_ref[s] * panel_cols + cols_ref[s]
                link[s] = head[b]
                head[b] = s

    for pair in range(panel_cols // 2):
        here = [head[block_row * panel_cols + 2 * pair + side] for side in range(2)]
        empty = (here[0] < 0) & (here[1] < 0)
        columns = slice(pair * 2 * tile, (pair + 1) * 2 * tile)

        @pl.when(empty)
        def _(columns=columns):
            out_ref[:, columns] = jnp.zeros((tile, 2 * tile), BF)

        @pl.when(jnp.logical_not(empty))
        def _(columns=columns, here=here):
            for side, s in enumerate(here):

                @pl.when(s < 0)
                def _(side=side):
                    acc[side] = jnp.zeros((tile, tile), F32)

                @pl.when(s >= 0)
                def _(side=side, s=s):
                    acc[side] = tiles_ref[s].astype(F32)

                    def more(t):
                        acc[side] += tiles_ref[t].astype(F32)
                        return link[t]

                    lax.while_loop(lambda t: t >= 0, more, link[s])

            both = jnp.concatenate([acc[0], acc[1]], axis=1)
            out_ref[:, columns] = both.astype(BF)


def build_panel(tiles, row_ids, col_ids, live, panel_rows, panel_cols):
    slots, tile, _ = tiles.shape
    smem = pl.BlockSpec(memory_space=pltpu.SMEM)
    return pl.pallas_call(
        functools.partial(build_kernel, slots, panel_cols, tile),
        grid=(panel_rows,),
        out_shape=jax.ShapeDtypeStruct((panel_rows * tile, panel_cols * tile), BF),
        in_specs=[smem, smem, smem, pl.BlockSpec((slots, tile, tile), lambda i: (0, 0, 0))],
        out_specs=pl.BlockSpec((tile, panel_cols * tile), lambda i: (i, 0)),
        scratch_shapes=[
            pltpu.SMEM((panel_rows * panel_cols,), jnp.int32),
            pltpu.SMEM((slots,), jnp.int32),
            pltpu.VMEM((2, tile, tile), F32),
        ],
        compiler_params=pltpu.CompilerParams(vmem_limit_bytes=32 * 2**20),
    )(row_ids, col_ids, live, tiles)


def filter_kernel(
    R, C, panel_ref, start_ref, center_ref, half_ref, out_ref, prev_ref,
    rowp, colp, sendr, sendc, sends, redr, redc, reds, mir, mine,
    ps_row, ps_sib, ps_col, pr_row, pr_col, rs_row, rs_sib, rs_col, rr_row, rr_sib, rr_col,
):
    w = start_ref.shape[1]
    w2 = 2 * w
    Z = C // 2
    r = lax.axis_index("row")
    c = lax.axis_index("col")
    z, core = c // 2, c % 2
    sib = c + 1 - 2 * core
    root_row = c * R // C
    off = c * R % C
    is_root = r == root_row
    not_root = r != root_row
    col_home = (r * C + c) // R
    col_slot = c % R

    def row_of(d):
        return (r + d) % R

    def chip(d):
        return 2 * ((z // 2 + d // 2) % (Z // 2)) + (z % 2 + d % 2) % 2

    def remote(src, dst, send_sem, recv_sem, row, col):
        return pltpu.make_async_remote_copy(
            src_ref=src, dst_ref=dst, send_sem=send_sem, recv_sem=recv_sem,
            device_id=(row, col), device_id_type=MESH,
        )

    barrier = pltpu.get_barrier_semaphore()
    pl.semaphore_signal(barrier, inc=1, device_id=(r, sib), device_id_type=MESH)
    for d in range(1, Z):
        pl.semaphore_signal(barrier, inc=1, device_id=(r, 2 * chip(d) + core), device_id_type=MESH)
    for d in range(1, R):
        pl.semaphore_signal(barrier, inc=1, device_id=(row_of(d), col_home), device_id_type=MESH)

    @pl.when(not_root)
    def _():
        for i in range(R):
            pl.semaphore_signal(barrier, inc=1, device_id=(root_row, off + i), device_id_type=MESH)

    pl.semaphore_wait(barrier, jnp.where(is_root, Z + R - 1, Z + 2 * R - 1))

    out_ref[...] = start_ref[...]
    prev_ref[...] = start_ref[...]

    def p_row(par, d):
        return remote(rowp.at[par, c], rowp.at[par, c], ps_row.at[d], pr_row.at[par, c], r, 2 * chip(d) + core)

    def p_in(par, src):
        return remote(rowp.at[par, src], rowp.at[par, src], ps_row.at[0], pr_row.at[par, src], r, src)

    def p_sib(par, d):
        src = 2 * chip(d) + core
        return remote(rowp.at[par, src], rowp.at[par, src], ps_sib.at[d], pr_row.at[par, src], r, sib)

    def p_col(par, d):
        return remote(rowp.at[par, c], colp.at[par, col_slot], ps_col.at[d], pr_col.at[par, col_slot], row_of(d), col_home)

    def p_col_in(par, i):
        return remote(colp.at[par, i], colp.at[par, i], ps_col.at[0], pr_col.at[par, i], root_row, off + i)

    def s_row(par, d):
        zz = chip(d)
        return remote(sendr.at[zz], redr.at[par, z], rs_row.at[d], rr_row.at[par, z], r, 2 * zz + core)

    def s_row_in(par, d):
        zz = chip(d)
        return remote(redr.at[par, zz], redr.at[par, zz], rs_row.at[0], rr_row.at[par, zz], r, 2 * zz + core)

    def s_sib(par, d):
        return remote(sends.at[d], reds.at[par, d], rs_sib.at[d], rr_sib.at[par, d], r, sib)

    def s_col(par, i):
        return remote(sendc.at[i], redc.at[par, r], rs_col.at[i], rr_col.at[par, r], root_row, off + i)

    def s_col_in(par, src):
        return remote(redc.at[par, src], redc.at[par, src], rs_col.at[0], rr_col.at[par, src], src, col_home)

    def wait_sums_sent(par):
        for d in range(1, Z):
            s_row(par, d).wait_send()
        for d in range(Z):
            s_sib(par, d).wait_send()

        @pl.when(not_root)
        def _():
            for i in range(R):
                s_col(par, i).wait_send()

    def step(k, carry):
        par = k % 2
        rowp[par, c] = out_ref[...].astype(BF)
        p_sib(par, 0).start()
        for d in range(Z - 1, 0, -1):
            p_row(par, d).start()
        for d in range(1, R):
            p_col(par, d).start()

        @pl.when(k > 0)
        def _():
            wait_sums_sent(1 - par)

        def arrive(d):
            p_in(par, 2 * chip(d) + core).wait_recv()
            p_sib(par, d).start()

        for d in range(Z):
            zz = chip(d)
            p_in(par, 2 * zz + 1 - core).wait_recv()
            lhs = jnp.concatenate([rowp[par, 2 * zz], rowp[par, 2 * zz + 1]], axis=1)
            part = jnp.dot(lhs, panel_ref[pl.ds(zz * w2, w2), :], preferred_element_type=F32)
            for i in range(R // 2):
                piece = part[:, i * w2 : (i + 1) * w2]
                if d == 0:
                    mir[i] = piece
                else:
                    mir[i] += piece
            if d == 0:
                arrive(1)
            if d + 2 < Z:
                arrive(d + 2)

        @pl.when(not_root)
        def _():
            for i in range(R):
                sendc[i] = mir[i // 2, :, (i % 2) * w : (i % 2 + 1) * w].astype(BF)
                s_col(par, i).start()
            for i in range(R):
                p_col_in(par, i).wait_recv()

        @pl.when(is_root)
        def _():
            for i in range(R):
                colp[par, i] = rowp[par, off + i]

        def pass_on(d):
            s_sib(par, d).wait_recv()
            sendr[chip(d)] = (mine[d] + reds[par, d]).astype(BF)
            s_row(par, d).start()

        x_col = jnp.concatenate([colp[par, i] for i in range(R)], axis=1)
        for d in range(Z - 1, -1, -1):
            zz = chip(d)
            part = lax.dot_general(
                x_col, panel_ref[pl.ds(zz * w2, w2), :], (((1,), (1,)), ((), ())),
                preferred_element_type=F32,
            )
            place = zz - off // 2
            inside = is_root & (place >= 0) & (place < R // 2)
            part = part + jnp.where(inside, mir[jnp.clip(place, 0, R // 2 - 1)], 0.0)
            left, right = part[:, :w], part[:, w:]
            sends[d] = jnp.where(core == 0, right, left)
            s_sib(par, d).start()
            mine[d] = jnp.where(core == 0, left, right)
            if d + 1 < Z:
                pass_on(d + 1)

        s_sib(par, 0).wait_recv()
        total = mine[0] + reds[par, 0]
        for d in range(1, R):
            s_col_in(par, row_of(d)).wait_recv()
            total = total + redc[par, row_of(d)].astype(F32)
        for d in range(1, Z):
            s_row_in(par, d).wait_recv()
            total = total + redr[par, chip(d)].astype(F32)

        first = k == 0
        scale = jnp.where(first, 1.0, 2.0)
        keep = jnp.where(first, 0.0, 1.0)
        current = out_ref[...]
        following = scale * (total - center_ref[0] * current) / half_ref[0] - keep * prev_ref[...]
        prev_ref[...] = current
        out_ref[...] = following
        for d in range(1, R):
            p_col(par, d).wait_send()
        for d in range(1, Z):
            p_row(par, d).wait_send()
        for d in range(Z):
            p_sib(par, d).wait_send()
        return carry

    lax.fori_loop(0, DEG, step, 0)
    wait_sums_sent((DEG - 1) % 2)


def body(R, C, start_block, center, half_width, matrix_tiles, tile_row, tile_col, tile_live):
    vectors, w = start_block.shape
    tile = matrix_tiles.shape[-1]
    own_clusters = w // tile
    panel = build_panel(
        matrix_tiles[0], tile_row[0], tile_col[0], tile_live[0], own_clusters * C, own_clusters * R
    )
    vmem = pl.BlockSpec(memory_space=pltpu.VMEM)
    smem = pl.BlockSpec(memory_space=pltpu.SMEM)
    dma = pltpu.SemaphoreType.DMA
    flat = jax.ShapeDtypeStruct((vectors, w), F32)
    Z = C // 2
    panel_bytes = panel.shape[0] * panel.shape[1] * 2
    return pl.pallas_call(
        functools.partial(filter_kernel, R, C),
        out_shape=(flat, flat),
        in_specs=[vmem, vmem, smem, smem],
        out_specs=(vmem, vmem),
        scratch_shapes=[
            pltpu.VMEM((2, C, vectors, w), BF),
            pltpu.VMEM((2, R, vectors, w), BF),
            pltpu.VMEM((Z, vectors, w), BF),
            pltpu.VMEM((R, vectors, w), BF),
            pltpu.VMEM((Z, vectors, w), F32),
            pltpu.VMEM((2, Z, vectors, w), BF),
            pltpu.VMEM((2, R, vectors, w), BF),
            pltpu.VMEM((2, Z, vectors, w), F32),
            pltpu.VMEM((R // 2, vectors, 2 * w), F32),
            pltpu.VMEM((Z, vectors, w), F32),
            dma((Z,)), dma((Z,)), dma((R,)), dma((2, C)), dma((2, R)),
            dma((Z,)), dma((Z,)), dma((R,)), dma((2, Z)), dma((2, Z)), dma((2, R)),
        ],
        compiler_params=pltpu.CompilerParams(
            collective_id=0, has_side_effects=True, vmem_limit_bytes=panel_bytes + 14 * 2**20
        ),
    )(panel, start_block, center, half_width)


def solution(mesh):
    R, C = mesh.shape["row"], mesh.shape["col"]
    in_specs = (
        P(None, ("row", "col")),
        P(),
        P(),
        P("row", "col", None, None),
        P("row", "col"),
        P("row", "col"),
        P("row", "col"),
    )
    out_specs = (P(None, ("row", "col")), P(None, ("row", "col")))
    return jax.shard_map(
        functools.partial(body, R, C), mesh=mesh, in_specs=in_specs, out_specs=out_specs, check_vma=False
    )
```

```python
import functools

import jax
import jax.numpy as jnp
from jax import lax
from jax.experimental import pallas as pl
from jax.experimental.pallas import tpu as pltpu
from jax.sharding import PartitionSpec as P

DEG = 8
MESH = pl.DeviceIdType.MESH
BF = jnp.bfloat16
F32 = jnp.float32


def build_kernel(slots, panel_cols, tile, rows_ref, cols_ref, live_ref, tiles_ref, out_ref, head, link, acc):
    block_row = pl.program_id(0)

    @pl.when(block_row == 0)
    def _():
        @pl.loop(0, pl.num_programs(0) * panel_cols)
        def _(b):
            head[b] = -1

        @pl.loop(0, slots)
        def _(s):
            @pl.when(live_ref[s] > 0)
            def _():
                b = rows_ref[s] * panel_cols + cols_ref[s]
                link[s] = head[b]
                head[b] = s

    for pair in range(panel_cols // 2):
        here = [head[block_row * panel_cols + 2 * pair + side] for side in range(2)]
        empty = (here[0] < 0) & (here[1] < 0)
        columns = slice(pair * 2 * tile, (pair + 1) * 2 * tile)

        @pl.when(empty)
        def _(columns=columns):
            out_ref[:, columns] = jnp.zeros((tile, 2 * tile), BF)

        @pl.when(jnp.logical_not(empty))
        def _(columns=columns, here=here):
            for side, s in enumerate(here):

                @pl.when(s < 0)
                def _(side=side):
                    acc[side] = jnp.zeros((tile, tile), F32)

                @pl.when(s >= 0)
                def _(side=side, s=s):
                    acc[side] = tiles_ref[s].astype(F32)

                    def more(t):
                        acc[side] += tiles_ref[t].astype(F32)
                        return link[t]

                    lax.while_loop(lambda t: t >= 0, more, link[s])

            both = jnp.concatenate([acc[0], acc[1]], axis=1)
            out_ref[:, columns] = both.astype(BF)


def build_panel(tiles, row_ids, col_ids, live, panel_rows, panel_cols):
    slots, tile, _ = tiles.shape
    smem = pl.BlockSpec(memory_space=pltpu.SMEM)
    return pl.pallas_call(
        functools.partial(build_kernel, slots, panel_cols, tile),
        grid=(panel_rows,),
        out_shape=jax.ShapeDtypeStruct((panel_rows * tile, panel_cols * tile), BF),
        in_specs=[smem, smem, smem, pl.BlockSpec((slots, tile, tile), lambda i: (0, 0, 0))],
        out_specs=pl.BlockSpec((tile, panel_cols * tile), lambda i: (i, 0)),
        scratch_shapes=[
            pltpu.SMEM((panel_rows * panel_cols,), jnp.int32),
            pltpu.SMEM((slots,), jnp.int32),
            pltpu.VMEM((2, tile, tile), F32),
        ],
        compiler_params=pltpu.CompilerParams(vmem_limit_bytes=32 * 2**20),
    )(row_ids, col_ids, live, tiles)


def filter_kernel(
    R, C, panel_ref, start_ref, center_ref, half_ref, out_ref, prev_ref,
    cur, old, land, zbuf, colp, rowp, sends, reds, sendr, redr, sendc, redc, mir,
    ex_send, ex_recv, pz_send, pz_recv, pc_send, pc_recv, pl_send, ps_send, pr_recv,
    ss_send, ss_recv, sr_send, sr_recv, sc_send, sc_recv,
):
    w = start_ref.shape[1]
    w2 = 2 * w
    H = R // 2
    me = lax.axis_index("row")
    c = lax.axis_index("col")
    z, core = c // 2, c % 2
    sib = c + 1 - 2 * core
    is_hub = me == z
    not_hub = me != z

    flat_home = me * C + c
    to_row, to_col = flat_home % R, flat_home // R
    flat_own = c * R + me
    from_row, from_col = flat_own // C, flat_own % C
    moved = flat_home != flat_own
    stays = flat_home == flat_own

    def turn(i, d):
        return (i + d) % R

    def at(chip):
        return 2 * chip + core

    def remote(src, dst, send_sem, recv_sem, row, col):
        return pltpu.make_async_remote_copy(
            src_ref=src, dst_ref=dst, send_sem=send_sem, recv_sem=recv_sem,
            device_id=(row, col), device_id_type=MESH,
        )

    barrier = pltpu.get_barrier_semaphore()

    def greet(row, col):
        pl.semaphore_signal(barrier, inc=1, device_id=(row, col), device_id_type=MESH)

    greet(me, sib)
    for d in range(1, R):
        greet(me, at(turn(z, d)))
        greet(turn(me, d), c)

    @pl.when(not_hub)
    def _():
        for d in range(1, R):
            greet(z, at(turn(z, d)))

    @pl.when(moved)
    def _():
        greet(to_row, to_col)
        greet(from_row, from_col)

    pl.semaphore_wait(
        barrier, 2 * R - 1 + jnp.where(not_hub, R - 1, 0) + jnp.where(moved, 2, 0)
    )

    def enter():
        return remote(start_ref, cur, ex_send.at[0], ex_recv.at[0], to_row, to_col)

    def leave(i):
        src = cur if i == 0 else old
        return remote(src, land.at[i], ex_send.at[1 + i], ex_recv.at[1 + i], from_row, from_col)

    @pl.when(moved)
    def _():
        enter().start()
        enter().wait()

    @pl.when(stays)
    def _():
        cur[...] = start_ref[...]

    old[...] = jnp.zeros_like(old)

    def p_z(par, d):
        return remote(zbuf.at[par, z], zbuf.at[par, z], pz_send.at[d], pz_recv.at[par, z], me, at(turn(z, d)))

    def p_z_in(par, d):
        src = turn(z, d)
        return remote(zbuf.at[par, src], zbuf.at[par, src], pz_send.at[d], pz_recv.at[par, src], me, at(src))

    def p_col(par, d):
        return remote(zbuf.at[par, z], colp.at[par, me], pc_send.at[d], pc_recv.at[par, me], turn(me, d), c)

    def p_col_in(par, d):
        src = turn(me, d)
        return remote(colp.at[par, src], colp.at[par, src], pc_send.at[d], pc_recv.at[par, src], src, c)

    def p_relay(par, d):
        src = turn(z, d)
        return remote(zbuf.at[par, src], rowp.at[par, core, me], pl_send.at[d], pr_recv.at[par, core, me], src, c)

    def p_in(par, half, piece):
        ref = rowp.at[par, half, piece]
        return remote(ref, ref, pl_send.at[0], pr_recv.at[par, half, piece], me, sib)

    def p_sib(par, piece):
        ref = rowp.at[par, core, piece]
        return remote(ref, ref, ps_send.at[piece], pr_recv.at[par, core, piece], me, sib)

    def s_sib(par, j):
        return remote(sends.at[j], reds.at[par, j], ss_send.at[j], ss_recv.at[par, j], me, sib)

    def s_row(par, i):
        return remote(sendr.at[i], redr.at[par, z], sr_send.at[i], sr_recv.at[par, z], i, at(me))

    def s_row_in(par, i):
        return remote(redr.at[par, i], redr.at[par, i], sr_send.at[0], sr_recv.at[par, i], z, at(i))

    def s_col(par, d):
        return remote(sendc.at[d], redc.at[par, me], sc_send.at[d], sc_recv.at[par, me], turn(me, d), c)

    def s_col_in(par, d):
        src = turn(me, d)
        return remote(redc.at[par, src], redc.at[par, src], sc_send.at[d], sc_recv.at[par, src], src, c)

    def wait_sums_sent(par):
        for j in range(H):
            s_sib(par, j).wait_send()
        for i in range(R):

            @pl.when(not_hub | (me != i))
            def _(i=i):
                s_row(par, i).wait_send()

        for d in range(1, R):
            s_col(par, d).wait_send()

    def direct(x_col, half, j):
        rows = panel_ref[pl.ds((half * H + j) * w2, w2), :]
        return lax.dot_general(x_col, rows, (((1,), (1,)), ((), ())), preferred_element_type=F32)

    def mirrored(par, half, j):
        lhs = jnp.concatenate([rowp[par, half, 2 * j], rowp[par, half, 2 * j + 1]], axis=1)
        rows = panel_ref[pl.ds((half * H + j) * w2, w2), :]
        return jnp.dot(lhs, rows, preferred_element_type=F32)

    def step(k, carry):
        par = k % 2
        rounded = cur[...].astype(BF)
        zbuf[par, z] = rounded
        colp[par, me] = rounded
        for d in range(1, R):
            p_col(par, d).start()
        for d in range(1, R):
            p_z(par, d).start()

        @pl.when(k > 0)
        def _():
            wait_sums_sent(1 - par)

        for d in range(1, R):
            p_col_in(par, d).wait_recv()

        @pl.when(is_hub)
        def _():
            for i in range(R):
                rowp[par, core, i] = colp[par, i]
                p_sib(par, i).start()

        x_col = jnp.concatenate([colp[par, i] for i in range(R)], axis=1)
        for j in range(H):
            sends[j] = direct(x_col, 1 - core, j)
            s_sib(par, j).start()

        for d in range(1, R):
            p_z_in(par, d).wait_recv()

            @pl.when(turn(z, d) != me)
            def _(d=d):
                p_relay(par, d).start()

        @pl.when(not_hub)
        def _():
            rowp[par, core, me] = zbuf[par, me]
            p_sib(par, me).start()

        for j in range(H):
            part = direct(x_col, core, j)
            s_sib(par, j).wait_recv()
            part = part + reds[par, j]
            for i in range(2 * j, 2 * j + 2):
                piece = part[:, (i - 2 * j) * w : (i - 2 * j + 1) * w].astype(BF)
                sendr[i] = piece

                @pl.when(not_hub | (me != i))
                def _(i=i):
                    s_row(par, i).start()

                @pl.when(is_hub & (me == i))
                def _(piece=piece):
                    redr[par, z] = piece

            if j == 0:

                @pl.when(not_hub)
                def _():
                    for d in range(1, R):
                        p_in(par, core, turn(me, d)).wait_recv()
                        p_sib(par, turn(me, d)).start()

        total = mirrored(par, core, 0)
        for j in range(1, H):
            total = total + mirrored(par, core, j)
        for j in range(H):
            for i in range(2 * j, 2 * j + 2):
                p_in(par, 1 - core, i).wait_recv()
            total = total + mirrored(par, 1 - core, j)
        for i in range(R):
            mir[i] = total[:, i * w : (i + 1) * w]
        for d in range(1, R):
            sendc[d] = mir[turn(me, d)].astype(BF)
            s_col(par, d).start()

        product = mir[me]
        for i in range(R):

            @pl.when(not_hub | (me != i))
            def _(i=i):
                s_row_in(par, i).wait_recv()

            product = product + redr[par, i].astype(F32)
        for d in range(1, R):
            s_col_in(par, d).wait_recv()
            product = product + redc[par, turn(me, d)].astype(F32)

        first = k == 0
        scale = jnp.where(first, 1.0, 2.0)
        keep = jnp.where(first, 0.0, 1.0)
        current = cur[...]
        following = scale * (product - center_ref[0] * current) / half_ref[0] - keep * old[...]
        old[...] = current
        cur[...] = following
        for d in range(1, R):
            p_col(par, d).wait_send()
            p_z(par, d).wait_send()

            @pl.when(turn(z, d) != me)
            def _(d=d):
                p_relay(par, d).wait_send()

        for i in range(R):
            p_sib(par, i).wait_send()
        return carry

    lax.fori_loop(0, DEG, step, 0)
    wait_sums_sent((DEG - 1) % 2)

    @pl.when(moved)
    def _():
        for i in range(2):
            leave(i).start()
        for i in range(2):
            leave(i).wait()
        out_ref[...] = land[0]
        prev_ref[...] = land[1]

    @pl.when(stays)
    def _():
        out_ref[...] = cur[...]
        prev_ref[...] = old[...]


def body(R, C, start_block, center, half_width, matrix_tiles, tile_row, tile_col, tile_live):
    vectors, w = start_block.shape
    tile = matrix_tiles.shape[-1]
    own_clusters = w // tile
    panel = build_panel(
        matrix_tiles[0], tile_row[0], tile_col[0], tile_live[0], own_clusters * C, own_clusters * R
    )
    vmem = pl.BlockSpec(memory_space=pltpu.VMEM)
    smem = pl.BlockSpec(memory_space=pltpu.SMEM)
    dma = pltpu.SemaphoreType.DMA
    flat = jax.ShapeDtypeStruct((vectors, w), F32)
    panel_bytes = panel.shape[0] * panel.shape[1] * 2
    return pl.pallas_call(
        functools.partial(filter_kernel, R, C),
        out_shape=(flat, flat),
        in_specs=[vmem, vmem, smem, smem],
        out_specs=(vmem, vmem),
        scratch_shapes=[
            pltpu.VMEM((vectors, w), F32),
            pltpu.VMEM((vectors, w), F32),
            pltpu.VMEM((2, vectors, w), F32),
            pltpu.VMEM((2, R, vectors, w), BF),
            pltpu.VMEM((2, R, vectors, w), BF),
            pltpu.VMEM((2, 2, R, vectors, w), BF),
            pltpu.VMEM((R // 2, vectors, 2 * w), F32),
            pltpu.VMEM((2, R // 2, vectors, 2 * w), F32),
            pltpu.VMEM((R, vectors, w), BF),
            pltpu.VMEM((2, R, vectors, w), BF),
            pltpu.VMEM((R, vectors, w), BF),
            pltpu.VMEM((2, R, vectors, w), BF),
            pltpu.VMEM((R, vectors, w), F32),
            dma((3,)), dma((3,)),
            dma((R,)), dma((2, R)), dma((R,)), dma((2, R)), dma((R,)), dma((R,)), dma((2, 2, R)),
            dma((R // 2,)), dma((2, R // 2)), dma((R,)), dma((2, R)), dma((R,)), dma((2, R)),
        ],
        compiler_params=pltpu.CompilerParams(
            collective_id=0, has_side_effects=True, vmem_limit_bytes=panel_bytes + 14 * 2**20
        ),
    )(panel, start_block, center, half_width)


def solution(mesh):
    R, C = mesh.shape["row"], mesh.shape["col"]
    assert C == 2 * R and R % 2 == 0
    in_specs = (
        P(None, ("row", "col")),
        P(),
        P(),
        P("row", "col", None, None),
        P("row", "col"),
        P("row", "col"),
        P("row", "col"),
    )
    out_specs = (P(None, ("row", "col")), P(None, ("row", "col")))
    return jax.shard_map(
        functools.partial(body, R, C), mesh=mesh, in_specs=in_specs, out_specs=out_specs, check_vma=False
    )
```

```python
import functools

import jax
import jax.numpy as jnp
from jax import lax
from jax.experimental import pallas as pl
from jax.experimental.pallas import tpu as pltpu
from jax.sharding import PartitionSpec as P

DEG = 8
MESH = pl.DeviceIdType.MESH
BF = jnp.bfloat16
F32 = jnp.float32


def build_kernel(slots, panel_cols, tile, flip, rows_ref, cols_ref, live_ref, tiles_ref, out_ref, head, link, acc):
    block_row = pl.program_id(0)

    def load(s):
        wide = tiles_ref[s].astype(F32)
        return wide.T if flip else wide

    @pl.when(block_row == 0)
    def _():
        @pl.loop(0, pl.num_programs(0) * panel_cols)
        def _(b):
            head[b] = -1

        @pl.loop(0, slots)
        def _(s):
            @pl.when(live_ref[s] > 0)
            def _():
                b = rows_ref[s] * panel_cols + cols_ref[s]
                link[s] = head[b]
                head[b] = s

    for pair in range(panel_cols // 2):
        here = [head[block_row * panel_cols + 2 * pair + side] for side in range(2)]
        empty = (here[0] < 0) & (here[1] < 0)
        columns = slice(pair * 2 * tile, (pair + 1) * 2 * tile)

        @pl.when(empty)
        def _(columns=columns):
            out_ref[:, columns] = jnp.zeros((tile, 2 * tile), BF)

        @pl.when(jnp.logical_not(empty))
        def _(columns=columns, here=here):
            for side, s in enumerate(here):

                @pl.when(s < 0)
                def _(side=side):
                    acc[side] = jnp.zeros((tile, tile), F32)

                @pl.when(s >= 0)
                def _(side=side, s=s):
                    acc[side] = load(s)

                    def more(t):
                        acc[side] += load(t)
                        return link[t]

                    lax.while_loop(lambda t: t >= 0, more, link[s])

            both = jnp.concatenate([acc[0], acc[1]], axis=1)
            out_ref[:, columns] = both.astype(BF)


def build_panel(tiles, row_ids, col_ids, live, panel_rows, panel_cols, flip=False):
    slots, tile, _ = tiles.shape
    smem = pl.BlockSpec(memory_space=pltpu.SMEM)
    return pl.pallas_call(
        functools.partial(build_kernel, slots, panel_cols, tile, flip),
        grid=(panel_rows,),
        out_shape=jax.ShapeDtypeStruct((panel_rows * tile, panel_cols * tile), BF),
        in_specs=[smem, smem, smem, pl.BlockSpec((slots, tile, tile), lambda i: (0, 0, 0))],
        out_specs=pl.BlockSpec((tile, panel_cols * tile), lambda i: (i, 0)),
        scratch_shapes=[
            pltpu.SMEM((panel_rows * panel_cols,), jnp.int32),
            pltpu.SMEM((slots,), jnp.int32),
            pltpu.VMEM((2, tile, tile), F32),
        ],
        compiler_params=pltpu.CompilerParams(vmem_limit_bytes=32 * 2**20),
    )(row_ids, col_ids, live, tiles)


def filter_kernel(
    R, C, both, panel_ref, flipped_ref, start_ref, center_ref, half_ref, out_ref, prev_ref,
    rowp, colp, sendr, sendc, sends, redr, redc, reds, mir, mine,
    ps_row, ps_sib, ps_col, pr_row, pr_col, rs_row, rs_sib, rs_col, rr_row, rr_sib, rr_col,
):
    w = start_ref.shape[1]
    w2 = 2 * w
    Z = C // 2
    r = lax.axis_index("row")
    c = lax.axis_index("col")
    z, core = c // 2, c % 2
    sib = c + 1 - 2 * core
    root_row = c * R // C
    off = c * R % C
    is_root = r == root_row
    not_root = r != root_row
    col_home = (r * C + c) // R
    col_slot = c % R

    def row_of(d):
        return (r + d) % R

    def chip(d):
        return 2 * ((z // 2 + d // 2) % (Z // 2)) + (z % 2 + d % 2) % 2

    def remote(src, dst, send_sem, recv_sem, row, col):
        return pltpu.make_async_remote_copy(
            src_ref=src, dst_ref=dst, send_sem=send_sem, recv_sem=recv_sem,
            device_id=(row, col), device_id_type=MESH,
        )

    barrier = pltpu.get_barrier_semaphore()
    pl.semaphore_signal(barrier, inc=1, device_id=(r, sib), device_id_type=MESH)
    for d in range(1, Z):
        pl.semaphore_signal(barrier, inc=1, device_id=(r, 2 * chip(d) + core), device_id_type=MESH)
    for d in range(1, R):
        pl.semaphore_signal(barrier, inc=1, device_id=(row_of(d), col_home), device_id_type=MESH)

    @pl.when(not_root)
    def _():
        for i in range(R):
            pl.semaphore_signal(barrier, inc=1, device_id=(root_row, off + i), device_id_type=MESH)

    pl.semaphore_wait(barrier, jnp.where(is_root, Z + R - 1, Z + 2 * R - 1))

    out_ref[...] = start_ref[...]
    prev_ref[...] = start_ref[...]

    def p_row(par, d):
        return remote(rowp.at[par, c], rowp.at[par, c], ps_row.at[d], pr_row.at[par, c], r, 2 * chip(d) + core)

    def p_in(par, src):
        return remote(rowp.at[par, src], rowp.at[par, src], ps_row.at[0], pr_row.at[par, src], r, src)

    def p_sib(par, d):
        src = 2 * chip(d) + core
        return remote(rowp.at[par, src], rowp.at[par, src], ps_sib.at[d], pr_row.at[par, src], r, sib)

    def p_col(par, d):
        return remote(rowp.at[par, c], colp.at[par, col_slot], ps_col.at[d], pr_col.at[par, col_slot], row_of(d), col_home)

    def p_col_in(par, i):
        return remote(colp.at[par, i], colp.at[par, i], ps_col.at[0], pr_col.at[par, i], root_row, off + i)

    def s_row(par, d):
        zz = chip(d)
        return remote(sendr.at[zz], redr.at[par, z], rs_row.at[d], rr_row.at[par, z], r, 2 * zz + core)

    def s_row_in(par, d):
        zz = chip(d)
        return remote(redr.at[par, zz], redr.at[par, zz], rs_row.at[0], rr_row.at[par, zz], r, 2 * zz + core)

    def s_sib(par, d):
        return remote(sends.at[d], reds.at[par, d], rs_sib.at[d], rr_sib.at[par, d], r, sib)

    def s_col(par, i):
        return remote(sendc.at[i], redc.at[par, r], rs_col.at[i], rr_col.at[par, r], root_row, off + i)

    def s_col_in(par, src):
        return remote(redc.at[par, src], redc.at[par, src], rs_col.at[0], rr_col.at[par, src], src, col_home)

    def wait_sums_sent(par):
        for d in range(1, Z):
            s_row(par, d).wait_send()
        for d in range(Z):
            s_sib(par, d).wait_send()

        @pl.when(not_root)
        def _():
            for i in range(R):
                s_col(par, i).wait_send()

    def step(k, carry):
        par = k % 2
        rowp[par, c] = out_ref[...].astype(BF)
        p_sib(par, 0).start()
        for d in range(Z - 1, 0, -1):
            p_row(par, d).start()
        for d in range(1, R):
            p_col(par, d).start()

        @pl.when(k > 0)
        def _():
            wait_sums_sent(1 - par)

        def arrive(d):
            p_in(par, 2 * chip(d) + core).wait_recv()
            p_sib(par, d).start()

        for d in range(Z):
            zz = chip(d)
            p_in(par, 2 * zz + 1 - core).wait_recv()
            lhs = jnp.concatenate([rowp[par, 2 * zz], rowp[par, 2 * zz + 1]], axis=1)
            part = jnp.dot(lhs, panel_ref[pl.ds(zz * w2, w2), :], preferred_element_type=F32)
            for i in range(R // 2):
                piece = part[:, i * w2 : (i + 1) * w2]
                if d == 0:
                    mir[i] = piece
                else:
                    mir[i] += piece
            if d == 0:
                arrive(1)
            if d + 2 < Z:
                arrive(d + 2)

        @pl.when(not_root)
        def _():
            for i in range(R):
                sendc[i] = mir[i // 2, :, (i % 2) * w : (i % 2 + 1) * w].astype(BF)
                s_col(par, i).start()
            for i in range(R):
                p_col_in(par, i).wait_recv()

        @pl.when(is_root)
        def _():
            for i in range(R):
                colp[par, i] = rowp[par, off + i]

        def pass_on(d):
            s_sib(par, d).wait_recv()
            sendr[chip(d)] = (mine[d] + reds[par, d]).astype(BF)
            s_row(par, d).start()

        x_col = jnp.concatenate([colp[par, i] for i in range(R)], axis=1)
        for d in range(Z - 1, -1, -1):
            zz = chip(d)
            if both:
                columns = pl.ds(pl.multiple_of(zz * w2, w2), w2)
                part = jnp.dot(x_col, flipped_ref[:, columns], preferred_element_type=F32)
            else:
                part = lax.dot_general(
                    x_col, panel_ref[pl.ds(zz * w2, w2), :], (((1,), (1,)), ((), ())),
                    preferred_element_type=F32,
                )
            place = zz - off // 2
            inside = is_root & (place >= 0) & (place < R // 2)
            part = part + jnp.where(inside, mir[jnp.clip(place, 0, R // 2 - 1)], 0.0)
            left, right = part[:, :w], part[:, w:]
            sends[d] = jnp.where(core == 0, right, left)
            s_sib(par, d).start()
            mine[d] = jnp.where(core == 0, left, right)
            if d + 1 < Z:
                pass_on(d + 1)

        s_sib(par, 0).wait_recv()
        total = mine[0] + reds[par, 0]
        for d in range(1, R):
            s_col_in(par, row_of(d)).wait_recv()
            total = total + redc[par, row_of(d)].astype(F32)
        for d in range(1, Z):
            s_row_in(par, d).wait_recv()
            total = total + redr[par, chip(d)].astype(F32)

        first = k == 0
        scale = jnp.where(first, 1.0, 2.0)
        keep = jnp.where(first, 0.0, 1.0)
        current = out_ref[...]
        following = scale * (total - center_ref[0] * current) / half_ref[0] - keep * prev_ref[...]
        prev_ref[...] = current
        out_ref[...] = following
        for d in range(1, R):
            p_col(par, d).wait_send()
        for d in range(1, Z):
            p_row(par, d).wait_send()
        for d in range(Z):
            p_sib(par, d).wait_send()
        return carry

    lax.fori_loop(0, DEG, step, 0)
    wait_sums_sent((DEG - 1) % 2)


def body(R, C, start_block, center, half_width, matrix_tiles, tile_row, tile_col, tile_live):
    vectors, w = start_block.shape
    tile = matrix_tiles.shape[-1]
    own_clusters = w // tile
    ids = (tile_row[0], tile_col[0])
    sizes = (own_clusters * C, own_clusters * R)
    panel = build_panel(matrix_tiles[0], *ids, tile_live[0], *sizes)
    both = 2 * panel.size * 2 <= 24 * 2**20
    if both:
        flipped = build_panel(matrix_tiles[0], *ids[::-1], tile_live[0], *sizes[::-1], flip=True)
    else:
        flipped = jnp.zeros((16, 128), BF)
    vmem = pl.BlockSpec(memory_space=pltpu.VMEM)
    smem = pl.BlockSpec(memory_space=pltpu.SMEM)
    dma = pltpu.SemaphoreType.DMA
    flat = jax.ShapeDtypeStruct((vectors, w), F32)
    Z = C // 2
    panel_bytes = (panel.size + flipped.size) * 2
    return pl.pallas_call(
        functools.partial(filter_kernel, R, C, both),
        out_shape=(flat, flat),
        in_specs=[vmem, vmem, vmem, smem, smem],
        out_specs=(vmem, vmem),
        scratch_shapes=[
            pltpu.VMEM((2, C, vectors, w), BF),
            pltpu.VMEM((2, R, vectors, w), BF),
            pltpu.VMEM((Z, vectors, w), BF),
            pltpu.VMEM((R, vectors, w), BF),
            pltpu.VMEM((Z, vectors, w), F32),
            pltpu.VMEM((2, Z, vectors, w), BF),
            pltpu.VMEM((2, R, vectors, w), BF),
            pltpu.VMEM((2, Z, vectors, w), F32),
            pltpu.VMEM((R // 2, vectors, 2 * w), F32),
            pltpu.VMEM((Z, vectors, w), F32),
            dma((Z,)), dma((Z,)), dma((R,)), dma((2, C)), dma((2, R)),
            dma((Z,)), dma((Z,)), dma((R,)), dma((2, Z)), dma((2, Z)), dma((2, R)),
        ],
        compiler_params=pltpu.CompilerParams(
            collective_id=0, has_side_effects=True, vmem_limit_bytes=panel_bytes + 14 * 2**20
        ),
    )(panel, flipped, start_block, center, half_width)


def solution(mesh):
    R, C = mesh.shape["row"], mesh.shape["col"]
    in_specs = (
        P(None, ("row", "col")),
        P(),
        P(),
        P("row", "col", None, None),
        P("row", "col"),
        P("row", "col"),
        P("row", "col"),
    )
    out_specs = (P(None, ("row", "col")), P(None, ("row", "col")))
    return jax.shard_map(
        functools.partial(body, R, C), mesh=mesh, in_specs=in_specs, out_specs=out_specs, check_vma=False
    )
```

```python
import functools

import jax
import jax.numpy as jnp
from jax import lax
from jax.experimental import pallas as pl
from jax.experimental.pallas import tpu as pltpu
from jax.sharding import PartitionSpec as P

DEG = 8
MESH = pl.DeviceIdType.MESH
BF = jnp.bfloat16
F32 = jnp.float32


def build_kernel(slots, panel_cols, tile, flip, rows_ref, cols_ref, live_ref, tiles_ref, out_ref, head, link, acc):
    block_row = pl.program_id(0)

    def load(s):
        wide = tiles_ref[s].astype(F32)
        return wide.T if flip else wide

    @pl.when(block_row == 0)
    def _():
        @pl.loop(0, pl.num_programs(0) * panel_cols)
        def _(b):
            head[b] = -1

        @pl.loop(0, slots)
        def _(s):
            @pl.when(live_ref[s] > 0)
            def _():
                b = rows_ref[s] * panel_cols + cols_ref[s]
                link[s] = head[b]
                head[b] = s

    for pair in range(panel_cols // 2):
        here = [head[block_row * panel_cols + 2 * pair + side] for side in range(2)]
        empty = (here[0] < 0) & (here[1] < 0)
        columns = slice(pair * 2 * tile, (pair + 1) * 2 * tile)

        @pl.when(empty)
        def _(columns=columns):
            out_ref[:, columns] = jnp.zeros((tile, 2 * tile), BF)

        @pl.when(jnp.logical_not(empty))
        def _(columns=columns, here=here):
            for side, s in enumerate(here):

                @pl.when(s < 0)
                def _(side=side):
                    acc[side] = jnp.zeros((tile, tile), F32)

                @pl.when(s >= 0)
                def _(side=side, s=s):
                    acc[side] = load(s)

                    def more(t):
                        acc[side] += load(t)
                        return link[t]

                    lax.while_loop(lambda t: t >= 0, more, link[s])

            both = jnp.concatenate([acc[0], acc[1]], axis=1)
            out_ref[:, columns] = both.astype(BF)


def build_panel(tiles, row_ids, col_ids, live, panel_rows, panel_cols, flip=False):
    slots, tile, _ = tiles.shape
    smem = pl.BlockSpec(memory_space=pltpu.SMEM)
    return pl.pallas_call(
        functools.partial(build_kernel, slots, panel_cols, tile, flip),
        grid=(panel_rows,),
        out_shape=jax.ShapeDtypeStruct((panel_rows * tile, panel_cols * tile), BF),
        in_specs=[smem, smem, smem, pl.BlockSpec((slots, tile, tile), lambda i: (0, 0, 0))],
        out_specs=pl.BlockSpec((tile, panel_cols * tile), lambda i: (i, 0)),
        scratch_shapes=[
            pltpu.SMEM((panel_rows * panel_cols,), jnp.int32),
            pltpu.SMEM((slots,), jnp.int32),
            pltpu.VMEM((2, tile, tile), F32),
        ],
        compiler_params=pltpu.CompilerParams(vmem_limit_bytes=32 * 2**20),
    )(row_ids, col_ids, live, tiles)


def filter_kernel(
    R, C, both, panel_ref, flipped_ref, start_ref, center_ref, half_ref, out_ref, prev_ref,
    cur, old, land, zbuf, colp, rowp, sends, reds, sendr, rbuf, redr, sendc, redc, mir,
    ex_send, ex_recv, pz_send, pz_recv, pc_send, pc_recv, pl_send, ps_send, pr_recv,
    ss_send, ss_recv, sx_send, sx_recv, sr_send, sr_recv, sc_send, sc_recv,
):
    w = start_ref.shape[1]
    w2 = 2 * w
    H = R // 2
    me = lax.axis_index("row")
    c = lax.axis_index("col")
    z, core = c // 2, c % 2
    sib = c + 1 - 2 * core
    is_hub = me == z
    not_hub = me != z

    flat_home = me * C + c
    to_row, to_col = flat_home % R, flat_home // R
    flat_own = c * R + me
    from_row, from_col = flat_own // C, flat_own % C
    moved = flat_home != flat_own
    stays = flat_home == flat_own

    def turn(i, d):
        return (i + d) % R

    def at(chip):
        return 2 * chip + core

    def remote(src, dst, send_sem, recv_sem, row, col):
        return pltpu.make_async_remote_copy(
            src_ref=src, dst_ref=dst, send_sem=send_sem, recv_sem=recv_sem,
            device_id=(row, col), device_id_type=MESH,
        )

    barrier = pltpu.get_barrier_semaphore()

    def greet(row, col):
        pl.semaphore_signal(barrier, inc=1, device_id=(row, col), device_id_type=MESH)

    greet(me, sib)
    for d in range(1, R):
        greet(me, at(turn(z, d)))
        greet(turn(me, d), c)

    @pl.when(moved)
    def _():
        greet(to_row, to_col)
        greet(from_row, from_col)

    pl.semaphore_wait(barrier, 2 * R - 1 + jnp.where(moved, 2, 0))

    def enter():
        return remote(start_ref, cur, ex_send.at[0], ex_recv.at[0], to_row, to_col)

    def leave(i):
        src = cur if i == 0 else old
        return remote(src, land.at[i], ex_send.at[1 + i], ex_recv.at[1 + i], from_row, from_col)

    @pl.when(moved)
    def _():
        enter().start()
        enter().wait()

    @pl.when(stays)
    def _():
        cur[...] = start_ref[...]

    old[...] = jnp.zeros_like(old)

    def p_z(par, d):
        return remote(zbuf.at[par, z], zbuf.at[par, z], pz_send.at[d], pz_recv.at[par, z], me, at(turn(z, d)))

    def p_z_in(par, d):
        src = turn(z, d)
        return remote(zbuf.at[par, src], zbuf.at[par, src], pz_send.at[d], pz_recv.at[par, src], me, at(src))

    def p_col(par, d):
        return remote(zbuf.at[par, z], colp.at[par, me], pc_send.at[d], pc_recv.at[par, me], turn(me, d), c)

    def p_col_in(par, d):
        src = turn(me, d)
        return remote(colp.at[par, src], colp.at[par, src], pc_send.at[d], pc_recv.at[par, src], src, c)

    def p_relay(par, d):
        src = turn(z, d)
        return remote(zbuf.at[par, src], rowp.at[par, core, me], pl_send.at[d], pr_recv.at[par, core, me], src, c)

    def p_in(par, half, piece):
        ref = rowp.at[par, half, piece]
        return remote(ref, ref, pl_send.at[0], pr_recv.at[par, half, piece], me, sib)

    def p_sib(par, piece):
        ref = rowp.at[par, core, piece]
        return remote(ref, ref, ps_send.at[piece], pr_recv.at[par, core, piece], me, sib)

    def s_sib(par, j):
        return remote(sends.at[j], reds.at[par, j], ss_send.at[j], ss_recv.at[par, j], me, sib)

    def s_plane(par, d):
        dst = turn(me, d)
        return remote(sendr.at[dst], rbuf.at[par, me], sx_send.at[d], sx_recv.at[par, me], dst, c)

    def s_plane_in(par, src):
        return remote(rbuf.at[par, src], rbuf.at[par, src], sx_send.at[0], sx_recv.at[par, src], src, c)

    def s_row(par, d):
        dst = turn(z, d)
        return remote(rbuf.at[par, dst], redr.at[par, z], sr_send.at[d], sr_recv.at[par, z], me, at(dst))

    def s_row_in(par, d):
        src = turn(z, d)
        return remote(redr.at[par, src], redr.at[par, src], sr_send.at[d], sr_recv.at[par, src], me, at(src))

    def s_col(par, d):
        return remote(sendc.at[d], redc.at[par, me], sc_send.at[d], sc_recv.at[par, me], turn(me, d), c)

    def s_col_in(par, d):
        src = turn(me, d)
        return remote(redc.at[par, src], redc.at[par, src], sc_send.at[d], sc_recv.at[par, src], src, c)

    def wait_sums_sent(par):
        for j in range(H):
            s_sib(par, j).wait_send()
        for d in range(1, R):
            s_plane(par, d).wait_send()
            s_row(par, d).wait_send()
            s_col(par, d).wait_send()

    def direct(x_col, half, j):
        place = pl.ds(pl.multiple_of((half * H + j) * w2, w2), w2)
        if both:
            return jnp.dot(x_col, flipped_ref[:, place], preferred_element_type=F32)
        rows = panel_ref[place, :]
        return lax.dot_general(x_col, rows, (((1,), (1,)), ((), ())), preferred_element_type=F32)

    def mirrored(par, half, j):
        lhs = jnp.concatenate([rowp[par, half, 2 * j], rowp[par, half, 2 * j + 1]], axis=1)
        rows = panel_ref[pl.ds((half * H + j) * w2, w2), :]
        return jnp.dot(lhs, rows, preferred_element_type=F32)

    def step(k, carry):
        par = k % 2
        rounded = cur[...].astype(BF)
        zbuf[par, z] = rounded
        colp[par, me] = rounded
        for d in range(1, R):
            p_col(par, d).start()
        for d in range(1, R):
            p_z(par, d).start()

        @pl.when(k > 0)
        def _():
            wait_sums_sent(1 - par)

        for d in range(1, R):
            p_col_in(par, d).wait_recv()

        @pl.when(is_hub)
        def _():
            for i in range(R):
                rowp[par, core, i] = colp[par, i]
                p_sib(par, i).start()

        x_col = jnp.concatenate([colp[par, i] for i in range(R)], axis=1)
        for j in range(H):
            sends[j] = direct(x_col, 1 - core, j)
            s_sib(par, j).start()

        for d in range(1, R):
            p_z_in(par, d).wait_recv()

            @pl.when(turn(z, d) != me)
            def _(d=d):
                p_relay(par, d).start()

        @pl.when(not_hub)
        def _():
            rowp[par, core, me] = zbuf[par, me]
            p_sib(par, me).start()

        for j in range(H):
            part = direct(x_col, core, j)
            s_sib(par, j).wait_recv()
            part = part + reds[par, j]
            for i in range(2 * j, 2 * j + 2):
                sendr[i] = part[:, (i - 2 * j) * w : (i - 2 * j + 1) * w].astype(BF)
            if j == 0:

                @pl.when(not_hub)
                def _():
                    for d in range(1, R):
                        p_in(par, core, turn(me, d)).wait_recv()
                        p_sib(par, turn(me, d)).start()

        rbuf[par, me] = sendr[me]
        for d in range(1, R):
            s_plane(par, d).start()

        total = mirrored(par, core, 0)
        for j in range(1, H):
            total = total + mirrored(par, core, j)

        for d in range(1, R):

            @pl.when(turn(z, d) != me)
            def _(d=d):
                s_plane_in(par, turn(z, d)).wait_recv()

            s_row(par, d).start()

        for j in range(H):
            for i in range(2 * j, 2 * j + 2):
                p_in(par, 1 - core, i).wait_recv()
            total = total + mirrored(par, 1 - core, j)
        for i in range(R):
            mir[i] = total[:, i * w : (i + 1) * w]
        for d in range(1, R):
            sendc[d] = mir[turn(me, d)].astype(BF)
            s_col(par, d).start()

        @pl.when(not_hub)
        def _():
            s_plane_in(par, z).wait_recv()

        product = mir[me] + rbuf[par, z].astype(F32)
        for d in range(1, R):
            s_row_in(par, d).wait_recv()
            product = product + redr[par, turn(z, d)].astype(F32)
        for d in range(1, R):
            s_col_in(par, d).wait_recv()
            product = product + redc[par, turn(me, d)].astype(F32)

        first = k == 0
        scale = jnp.where(first, 1.0, 2.0)
        keep = jnp.where(first, 0.0, 1.0)
        current = cur[...]
        following = scale * (product - center_ref[0] * current) / half_ref[0] - keep * old[...]
        old[...] = current
        cur[...] = following
        for d in range(1, R):
            p_col(par, d).wait_send()
            p_z(par, d).wait_send()

            @pl.when(turn(z, d) != me)
            def _(d=d):
                p_relay(par, d).wait_send()

        for i in range(R):
            p_sib(par, i).wait_send()
        return carry

    lax.fori_loop(0, DEG, step, 0)
    wait_sums_sent((DEG - 1) % 2)

    @pl.when(moved)
    def _():
        for i in range(2):
            leave(i).start()
        for i in range(2):
            leave(i).wait()
        out_ref[...] = land[0]
        prev_ref[...] = land[1]

    @pl.when(stays)
    def _():
        out_ref[...] = cur[...]
        prev_ref[...] = old[...]


def body(R, C, start_block, center, half_width, matrix_tiles, tile_row, tile_col, tile_live):
    vectors, w = start_block.shape
    tile = matrix_tiles.shape[-1]
    own_clusters = w // tile
    ids = (tile_row[0], tile_col[0])
    sizes = (own_clusters * C, own_clusters * R)
    panel = build_panel(matrix_tiles[0], *ids, tile_live[0], *sizes)
    both = 2 * panel.size * 2 <= 24 * 2**20
    if both:
        flipped = build_panel(matrix_tiles[0], *ids[::-1], tile_live[0], *sizes[::-1], flip=True)
    else:
        flipped = jnp.zeros((16, 128), BF)
    vmem = pl.BlockSpec(memory_space=pltpu.VMEM)
    smem = pl.BlockSpec(memory_space=pltpu.SMEM)
    dma = pltpu.SemaphoreType.DMA
    flat = jax.ShapeDtypeStruct((vectors, w), F32)
    panel_bytes = (panel.size + flipped.size) * 2
    return pl.pallas_call(
        functools.partial(filter_kernel, R, C, both),
        out_shape=(flat, flat),
        in_specs=[vmem, vmem, vmem, smem, smem],
        out_specs=(vmem, vmem),
        scratch_shapes=[
            pltpu.VMEM((vectors, w), F32),
            pltpu.VMEM((vectors, w), F32),
            pltpu.VMEM((2, vectors, w), F32),
            pltpu.VMEM((2, R, vectors, w), BF),
            pltpu.VMEM((2, R, vectors, w), BF),
            pltpu.VMEM((2, 2, R, vectors, w), BF),
            pltpu.VMEM((R // 2, vectors, 2 * w), F32),
            pltpu.VMEM((2, R // 2, vectors, 2 * w), F32),
            pltpu.VMEM((R, vectors, w), BF),
            pltpu.VMEM((2, R, vectors, w), BF),
            pltpu.VMEM((2, R, vectors, w), BF),
            pltpu.VMEM((R, vectors, w), BF),
            pltpu.VMEM((2, R, vectors, w), BF),
            pltpu.VMEM((R, vectors, w), F32),
            dma((3,)), dma((3,)),
            dma((R,)), dma((2, R)), dma((R,)), dma((2, R)), dma((R,)), dma((R,)), dma((2, 2, R)),
            dma((R // 2,)), dma((2, R // 2)), dma((R,)), dma((2, R)), dma((R,)), dma((2, R)), dma((R,)), dma((2, R)),
        ],
        compiler_params=pltpu.CompilerParams(
            collective_id=0, has_side_effects=True, vmem_limit_bytes=panel_bytes + 14 * 2**20
        ),
    )(panel, flipped, start_block, center, half_width)


def solution(mesh):
    R, C = mesh.shape["row"], mesh.shape["col"]
    assert C == 2 * R and R % 2 == 0
    in_specs = (
        P(None, ("row", "col")),
        P(),
        P(),
        P("row", "col", None, None),
        P("row", "col"),
        P("row", "col"),
        P("row", "col"),
    )
    out_specs = (P(None, ("row", "col")), P(None, ("row", "col")))
    return jax.shard_map(
        functools.partial(body, R, C), mesh=mesh, in_specs=in_specs, out_specs=out_specs, check_vma=False
    )
```

```python
import functools

import jax
import jax.numpy as jnp
from jax import lax
from jax.experimental import pallas as pl
from jax.experimental.pallas import tpu as pltpu
from jax.sharding import PartitionSpec as P

DEG = 8
MESH = pl.DeviceIdType.MESH
BF = jnp.bfloat16
F32 = jnp.float32


def build_kernel(slots, panel_cols, tile, flip, rows_ref, cols_ref, live_ref, tiles_ref, out_ref, head, link, acc):
    block_row = pl.program_id(0)

    def load(s):
        wide = tiles_ref[s].astype(F32)
        return wide.T if flip else wide

    @pl.when(block_row == 0)
    def _():
        @pl.loop(0, pl.num_programs(0) * panel_cols)
        def _(b):
            head[b] = -1

        @pl.loop(0, slots)
        def _(s):
            @pl.when(live_ref[s] > 0)
            def _():
                b = rows_ref[s] * panel_cols + cols_ref[s]
                link[s] = head[b]
                head[b] = s

    for pair in range(panel_cols // 2):
        here = [head[block_row * panel_cols + 2 * pair + side] for side in range(2)]
        empty = (here[0] < 0) & (here[1] < 0)
        columns = slice(pair * 2 * tile, (pair + 1) * 2 * tile)

        @pl.when(empty)
        def _(columns=columns):
            out_ref[:, columns] = jnp.zeros((tile, 2 * tile), BF)

        @pl.when(jnp.logical_not(empty))
        def _(columns=columns, here=here):
            for side, s in enumerate(here):

                @pl.when(s < 0)
                def _(side=side):
                    acc[side] = jnp.zeros((tile, tile), F32)

                @pl.when(s >= 0)
                def _(side=side, s=s):
                    acc[side] = load(s)

                    def more(t):
                        acc[side] += load(t)
                        return link[t]

                    lax.while_loop(lambda t: t >= 0, more, link[s])

            both = jnp.concatenate([acc[0], acc[1]], axis=1)
            out_ref[:, columns] = both.astype(BF)


def build_panel(tiles, row_ids, col_ids, live, panel_rows, panel_cols, flip=False):
    slots, tile, _ = tiles.shape
    smem = pl.BlockSpec(memory_space=pltpu.SMEM)
    return pl.pallas_call(
        functools.partial(build_kernel, slots, panel_cols, tile, flip),
        grid=(panel_rows,),
        out_shape=jax.ShapeDtypeStruct((panel_rows * tile, panel_cols * tile), BF),
        in_specs=[smem, smem, smem, pl.BlockSpec((slots, tile, tile), lambda i: (0, 0, 0))],
        out_specs=pl.BlockSpec((tile, panel_cols * tile), lambda i: (i, 0)),
        scratch_shapes=[
            pltpu.SMEM((panel_rows * panel_cols,), jnp.int32),
            pltpu.SMEM((slots,), jnp.int32),
            pltpu.VMEM((2, tile, tile), F32),
        ],
        compiler_params=pltpu.CompilerParams(vmem_limit_bytes=32 * 2**20),
    )(row_ids, col_ids, live, tiles)


def filter_kernel(
    R, C, both, panel_ref, flipped_ref, start_ref, center_ref, half_ref, out_ref, prev_ref,
    rowp, colp, sendr, sendc, sends, redr, redc, reds, mine,
    ps_row, ps_sib, ps_col, pr_row, pr_col, rs_row, rs_sib, rs_col, rr_row, rr_sib, rr_col,
):
    w = start_ref.shape[1]
    w2 = 2 * w
    Z = C // 2
    r = lax.axis_index("row")
    c = lax.axis_index("col")
    z, core = c // 2, c % 2
    sib = c + 1 - 2 * core
    root_row = c * R // C
    off = c * R % C
    col_home = (r * C + c) // R
    col_slot = c % R
    stays = col_home == c
    leaves = col_home != c

    def row_of(d):
        return (r + d) % R

    def chip(d):
        return 2 * ((z // 2 + d // 2) % (Z // 2)) + (z % 2 + d % 2) % 2

    def remote(src, dst, send_sem, recv_sem, row, col):
        return pltpu.make_async_remote_copy(
            src_ref=src, dst_ref=dst, send_sem=send_sem, recv_sem=recv_sem,
            device_id=(row, col), device_id_type=MESH,
        )

    barrier = pltpu.get_barrier_semaphore()
    pl.semaphore_signal(barrier, inc=1, device_id=(r, sib), device_id_type=MESH)
    for d in range(1, Z):
        pl.semaphore_signal(barrier, inc=1, device_id=(r, 2 * chip(d) + core), device_id_type=MESH)
    for d in range(R):

        @pl.when(leaves | (d != 0))
        def _(d=d):
            pl.semaphore_signal(barrier, inc=1, device_id=(row_of(d), col_home), device_id_type=MESH)

    for i in range(R):

        @pl.when(leaves | (col_slot != i))
        def _(i=i):
            pl.semaphore_signal(barrier, inc=1, device_id=(root_row, off + i), device_id_type=MESH)

    pl.semaphore_wait(barrier, jnp.where(stays, Z + 2 * R - 2, Z + 2 * R))

    out_ref[...] = start_ref[...]
    prev_ref[...] = start_ref[...]

    def p_row(par, d):
        return remote(rowp.at[par, c], rowp.at[par, c], ps_row.at[d], pr_row.at[par, c], r, 2 * chip(d) + core)

    def p_in(par, src):
        return remote(rowp.at[par, src], rowp.at[par, src], ps_row.at[0], pr_row.at[par, src], r, src)

    def p_sib(par, d):
        src = 2 * chip(d) + core
        return remote(rowp.at[par, src], rowp.at[par, src], ps_sib.at[d], pr_row.at[par, src], r, sib)

    def p_col(par, d):
        return remote(rowp.at[par, c], colp.at[par, col_slot], ps_col.at[d], pr_col.at[par, col_slot], row_of(d), col_home)

    def p_col_in(par, i):
        return remote(colp.at[par, i], colp.at[par, i], ps_col.at[0], pr_col.at[par, i], root_row, off + i)

    def s_row(par, d):
        zz = chip(d)
        return remote(sendr.at[zz], redr.at[par, z], rs_row.at[d], rr_row.at[par, z], r, 2 * zz + core)

    def s_row_in(par, d):
        zz = chip(d)
        return remote(redr.at[par, zz], redr.at[par, zz], rs_row.at[0], rr_row.at[par, zz], r, 2 * zz + core)

    def s_sib(par, d):
        return remote(sends.at[d], reds.at[par, d], rs_sib.at[d], rr_sib.at[par, d], r, sib)

    def s_col(par, i):
        return remote(sendc.at[i], redc.at[par, r], rs_col.at[i], rr_col.at[par, r], root_row, off + i)

    def s_col_in(par, src):
        return remote(redc.at[par, src], redc.at[par, src], rs_col.at[0], rr_col.at[par, src], src, col_home)

    def wait_sums_sent(par):
        for d in range(1, Z):
            s_row(par, d).wait_send()
        for d in range(Z):
            s_sib(par, d).wait_send()

        for i in range(R):

            @pl.when(leaves | (col_slot != i))
            def _(i=i):
                s_col(par, i).wait_send()

    def step(k, carry):
        par = k % 2
        rounded = out_ref[...].astype(BF)
        rowp[par, c] = rounded
        for d in range(1, R):
            p_col(par, d).start()

        @pl.when(leaves)
        def _():
            p_col(par, 0).start()

        @pl.when(stays)
        def _():
            colp[par, col_slot] = rounded

        for d in range(Z - 1, 0, -1):
            p_row(par, d).start()
        p_sib(par, 0).start()

        @pl.when(k > 0)
        def _():
            wait_sums_sent(1 - par)

        for i in range(R):

            @pl.when(leaves | (col_slot != i))
            def _(i=i):
                p_col_in(par, i).wait_recv()

        def pass_on(d):
            s_sib(par, d).wait_recv()
            sendr[chip(d)] = (mine[d] + reds[par, d]).astype(BF)
            s_row(par, d).start()

        x_col = jnp.concatenate([colp[par, i] for i in range(R)], axis=1)
        for d in range(Z - 1, -1, -1):
            zz = chip(d)
            if both:
                columns = pl.ds(pl.multiple_of(zz * w2, w2), w2)
                part = jnp.dot(x_col, flipped_ref[:, columns], preferred_element_type=F32)
            else:
                part = lax.dot_general(
                    x_col, panel_ref[pl.ds(zz * w2, w2), :], (((1,), (1,)), ((), ())),
                    preferred_element_type=F32,
                )
            left, right = part[:, :w], part[:, w:]
            sends[d] = jnp.where(core == 0, right, left)
            s_sib(par, d).start()
            mine[d] = jnp.where(core == 0, left, right)
            if d == Z - 1:
                for e in range(1, Z):
                    p_in(par, 2 * chip(e) + core).wait_recv()
                    p_sib(par, e).start()
            if d + 2 < Z:
                pass_on(d + 2)

        total = None
        for d in range(Z):
            zz = chip(d)
            p_in(par, 2 * zz + 1 - core).wait_recv()
            lhs = jnp.concatenate([rowp[par, 2 * zz], rowp[par, 2 * zz + 1]], axis=1)
            part = jnp.dot(lhs, panel_ref[pl.ds(zz * w2, w2), :], preferred_element_type=F32)
            total = part if d == 0 else total + part
            if d == 0:
                pass_on(1)

        for i in range(R):
            sendc[i] = total[:, i * w : (i + 1) * w].astype(BF)

            @pl.when(leaves | (col_slot != i))
            def _(i=i):
                s_col(par, i).start()

        @pl.when(stays)
        def _():
            redc[par, r] = sendc[col_slot]

        s_sib(par, 0).wait_recv()
        product = mine[0] + reds[par, 0]
        for d in range(1, Z):
            s_row_in(par, d).wait_recv()
            product = product + redr[par, chip(d)].astype(F32)
        for d in range(R):
            if d == 0:

                @pl.when(leaves)
                def _():
                    s_col_in(par, r).wait_recv()

            else:
                s_col_in(par, row_of(d)).wait_recv()
            product = product + redc[par, row_of(d)].astype(F32)

        first = k == 0
        scale = jnp.where(first, 1.0, 2.0)
        keep = jnp.where(first, 0.0, 1.0)
        current = out_ref[...]
        following = scale * (product - center_ref[0] * current) / half_ref[0] - keep * prev_ref[...]
        prev_ref[...] = current
        out_ref[...] = following
        for d in range(1, R):
            p_col(par, d).wait_send()

        @pl.when(leaves)
        def _():
            p_col(par, 0).wait_send()

        for d in range(1, Z):
            p_row(par, d).wait_send()
        for d in range(Z):
            p_sib(par, d).wait_send()
        return carry

    lax.fori_loop(0, DEG, step, 0)
    wait_sums_sent((DEG - 1) % 2)


def body(R, C, start_block, center, half_width, matrix_tiles, tile_row, tile_col, tile_live):
    vectors, w = start_block.shape
    tile = matrix_tiles.shape[-1]
    own_clusters = w // tile
    ids = (tile_row[0], tile_col[0])
    sizes = (own_clusters * C, own_clusters * R)
    panel = build_panel(matrix_tiles[0], *ids, tile_live[0], *sizes)
    both = 2 * panel.size * 2 <= 24 * 2**20
    if both:
        flipped = build_panel(matrix_tiles[0], *ids[::-1], tile_live[0], *sizes[::-1], flip=True)
    else:
        flipped = jnp.zeros((16, 128), BF)
    vmem = pl.BlockSpec(memory_space=pltpu.VMEM)
    smem = pl.BlockSpec(memory_space=pltpu.SMEM)
    dma = pltpu.SemaphoreType.DMA
    flat = jax.ShapeDtypeStruct((vectors, w), F32)
    Z = C // 2
    panel_bytes = (panel.size + flipped.size) * 2
    return pl.pallas_call(
        functools.partial(filter_kernel, R, C, both),
        out_shape=(flat, flat),
        in_specs=[vmem, vmem, vmem, smem, smem],
        out_specs=(vmem, vmem),
        scratch_shapes=[
            pltpu.VMEM((2, C, vectors, w), BF),
            pltpu.VMEM((2, R, vectors, w), BF),
            pltpu.VMEM((Z, vectors, w), BF),
            pltpu.VMEM((R, vectors, w), BF),
            pltpu.VMEM((Z, vectors, w), F32),
            pltpu.VMEM((2, Z, vectors, w), BF),
            pltpu.VMEM((2, R, vectors, w), BF),
            pltpu.VMEM((2, Z, vectors, w), F32),
            pltpu.VMEM((Z, vectors, w), F32),
            dma((Z,)), dma((Z,)), dma((R,)), dma((2, C)), dma((2, R)),
            dma((Z,)), dma((Z,)), dma((R,)), dma((2, Z)), dma((2, Z)), dma((2, R)),
        ],
        compiler_params=pltpu.CompilerParams(
            collective_id=0, has_side_effects=True, vmem_limit_bytes=panel_bytes + 14 * 2**20
        ),
    )(panel, flipped, start_block, center, half_width)


def solution(mesh):
    R, C = mesh.shape["row"], mesh.shape["col"]
    in_specs = (
        P(None, ("row", "col")),
        P(),
        P(),
        P("row", "col", None, None),
        P("row", "col"),
        P("row", "col"),
        P("row", "col"),
    )
    out_specs = (P(None, ("row", "col")), P(None, ("row", "col")))
    return jax.shard_map(
        functools.partial(body, R, C), mesh=mesh, in_specs=in_specs, out_specs=out_specs, check_vma=False
    )
```

```python
import functools

import jax
import jax.numpy as jnp
from jax import lax
from jax.experimental import pallas as pl
from jax.experimental.pallas import tpu as pltpu
from jax.sharding import PartitionSpec as P

DEG = 8
MESH = pl.DeviceIdType.MESH
BF = jnp.bfloat16
F32 = jnp.float32


def build_kernel(slots, panel_cols, tile, flip, rows_ref, cols_ref, live_ref, tiles_ref, out_ref, head, link, acc):
    per_step = out_ref.shape[0] // tile
    step = pl.program_id(0)

    def load(s):
        wide = tiles_ref[s].astype(F32)
        return wide.T if flip else wide

    @pl.when(step == 0)
    def _():
        @pl.loop(0, pl.num_programs(0) * per_step * panel_cols)
        def _(b):
            head[b] = -1

        @pl.loop(0, slots)
        def _(s):
            @pl.when(live_ref[s] > 0)
            def _():
                b = rows_ref[s] * panel_cols + cols_ref[s]
                link[s] = head[b]
                head[b] = s

    @pl.loop(0, per_step)
    def _(local):
        block_row = step * per_step + local
        rows = pl.ds(pl.multiple_of(local * tile, tile), tile)
        for pair in range(panel_cols // 2):
            here = [head[block_row * panel_cols + 2 * pair + side] for side in range(2)]
            empty = (here[0] < 0) & (here[1] < 0)
            columns = slice(pair * 2 * tile, (pair + 1) * 2 * tile)

            @pl.when(empty)
            def _(columns=columns):
                out_ref[rows, columns] = jnp.zeros((tile, 2 * tile), BF)

            @pl.when(jnp.logical_not(empty))
            def _(columns=columns, here=here):
                for side, s in enumerate(here):

                    @pl.when(s < 0)
                    def _(side=side):
                        acc[side] = jnp.zeros((tile, tile), F32)

                    @pl.when(s >= 0)
                    def _(side=side, s=s):
                        acc[side] = load(s)

                        def more(t):
                            acc[side] += load(t)
                            return link[t]

                        lax.while_loop(lambda t: t >= 0, more, link[s])

                both = jnp.concatenate([acc[0], acc[1]], axis=1)
                out_ref[rows, columns] = both.astype(BF)


def build_panel(tiles, row_ids, col_ids, live, panel_rows, panel_cols, flip=False):
    slots, tile, _ = tiles.shape
    per_step = 4
    smem = pl.BlockSpec(memory_space=pltpu.SMEM)
    return pl.pallas_call(
        functools.partial(build_kernel, slots, panel_cols, tile, flip),
        grid=(panel_rows // per_step,),
        out_shape=jax.ShapeDtypeStruct((panel_rows * tile, panel_cols * tile), BF),
        in_specs=[smem, smem, smem, pl.BlockSpec((slots, tile, tile), lambda i: (0, 0, 0))],
        out_specs=pl.BlockSpec((per_step * tile, panel_cols * tile), lambda i: (i, 0)),
        scratch_shapes=[
            pltpu.SMEM((panel_rows * panel_cols,), jnp.int32),
            pltpu.SMEM((slots,), jnp.int32),
            pltpu.VMEM((2, tile, tile), F32),
        ],
        compiler_params=pltpu.CompilerParams(vmem_limit_bytes=28 * 2**20),
    )(row_ids, col_ids, live, tiles)


def filter_kernel(
    R, C, both, panel_ref, flipped_ref, start_ref, center_ref, half_ref, out_ref, prev_ref,
    rowp, colp, sendr, sendc, sends, redr, redc, reds, mir, mine,
    ps_row, ps_sib, ps_col, pr_row, pr_col, rs_row, rs_sib, rs_col, rr_row, rr_sib, rr_col,
):
    w = start_ref.shape[1]
    w2 = 2 * w
    Z = C // 2
    r = lax.axis_index("row")
    c = lax.axis_index("col")
    z, core = c // 2, c % 2
    sib = c + 1 - 2 * core
    root_row = c * R // C
    off = c * R % C
    is_root = r == root_row
    not_root = r != root_row
    col_home = (r * C + c) // R
    col_slot = c % R

    def row_of(d):
        return (r + d) % R

    def chip(d):
        return 2 * ((z // 2 + d // 2) % (Z // 2)) + (z % 2 + d % 2) % 2

    def remote(src, dst, send_sem, recv_sem, row, col):
        return pltpu.make_async_remote_copy(
            src_ref=src, dst_ref=dst, send_sem=send_sem, recv_sem=recv_sem,
            device_id=(row, col), device_id_type=MESH,
        )

    barrier = pltpu.get_barrier_semaphore()
    pl.semaphore_signal(barrier, inc=1, device_id=(r, sib), device_id_type=MESH)
    for d in range(1, Z):
        pl.semaphore_signal(barrier, inc=1, device_id=(r, 2 * chip(d) + core), device_id_type=MESH)
    for d in range(1, R):
        pl.semaphore_signal(barrier, inc=1, device_id=(row_of(d), col_home), device_id_type=MESH)

    @pl.when(not_root)
    def _():
        for i in range(R):
            pl.semaphore_signal(barrier, inc=1, device_id=(root_row, off + i), device_id_type=MESH)

    pl.semaphore_wait(barrier, jnp.where(is_root, Z + R - 1, Z + 2 * R - 1))

    out_ref[...] = start_ref[...]
    prev_ref[...] = start_ref[...]

    def p_row(par, d):
        return remote(rowp.at[par, c], rowp.at[par, c], ps_row.at[d], pr_row.at[par, c], r, 2 * chip(d) + core)

    def p_in(par, src):
        return remote(rowp.at[par, src], rowp.at[par, src], ps_row.at[0], pr_row.at[par, src], r, src)

    def p_sib(par, d):
        src = 2 * chip(d) + core
        return remote(rowp.at[par, src], rowp.at[par, src], ps_sib.at[d], pr_row.at[par, src], r, sib)

    def p_col(par, d):
        return remote(rowp.at[par, c], colp.at[par, col_slot], ps_col.at[d], pr_col.at[par, col_slot], row_of(d), col_home)

    def p_col_in(par, i):
        return remote(colp.at[par, i], colp.at[par, i], ps_col.at[0], pr_col.at[par, i], root_row, off + i)

    def s_row(par, d):
        zz = chip(d)
        return remote(sendr.at[zz], redr.at[par, z], rs_row.at[d], rr_row.at[par, z], r, 2 * zz + core)

    def s_row_in(par, d):
        zz = chip(d)
        return remote(redr.at[par, zz], redr.at[par, zz], rs_row.at[0], rr_row.at[par, zz], r, 2 * zz + core)

    def s_sib(par, d):
        return remote(sends.at[d], reds.at[par, d], rs_sib.at[d], rr_sib.at[par, d], r, sib)

    def s_col(par, i):
        return remote(sendc.at[i], redc.at[par, r], rs_col.at[i], rr_col.at[par, r], root_row, off + i)

    def s_col_in(par, src):
        return remote(redc.at[par, src], redc.at[par, src], rs_col.at[0], rr_col.at[par, src], src, col_home)

    def wait_sums_sent(par):
        for d in range(1, Z):
            s_row(par, d).wait_send()
        for d in range(Z):
            s_sib(par, d).wait_send()

        @pl.when(not_root)
        def _():
            for i in range(R):
                s_col(par, i).wait_send()

    def step(k, carry):
        par = k % 2
        rowp[par, c] = out_ref[...].astype(BF)
        p_sib(par, 0).start()
        for d in range(Z - 1, 0, -1):
            p_row(par, d).start()
        for d in range(1, R):
            p_col(par, d).start()

        @pl.when(k > 0)
        def _():
            wait_sums_sent(1 - par)

        def arrive(d):
            p_in(par, 2 * chip(d) + core).wait_recv()
            p_sib(par, d).start()

        for d in range(Z):
            zz = chip(d)
            p_in(par, 2 * zz + 1 - core).wait_recv()
            lhs = jnp.concatenate([rowp[par, 2 * zz], rowp[par, 2 * zz + 1]], axis=1)
            part = jnp.dot(lhs, panel_ref[pl.ds(zz * w2, w2), :], preferred_element_type=F32)
            for i in range(R // 2):
                piece = part[:, i * w2 : (i + 1) * w2]
                if d == 0:
                    mir[i] = piece
                else:
                    mir[i] += piece
            if d == 0:
                arrive(1)
            if d + 2 < Z:
                arrive(d + 2)

        @pl.when(not_root)
        def _():
            for i in range(R):
                sendc[i] = mir[i // 2, :, (i % 2) * w : (i % 2 + 1) * w].astype(BF)
                s_col(par, i).start()
            for i in range(R):
                p_col_in(par, i).wait_recv()

        @pl.when(is_root)
        def _():
            for i in range(R):
                colp[par, i] = rowp[par, off + i]

        def pass_on(d):
            s_sib(par, d).wait_recv()
            sendr[chip(d)] = (mine[d] + reds[par, d]).astype(BF)
            s_row(par, d).start()

        x_col = jnp.concatenate([colp[par, i] for i in range(R)], axis=1)
        for d in range(Z - 1, -1, -1):
            zz = chip(d)
            if both:
                columns = pl.ds(pl.multiple_of(zz * w2, w2), w2)
                part = jnp.dot(x_col, flipped_ref[:, columns], preferred_element_type=F32)
            else:
                part = lax.dot_general(
                    x_col, panel_ref[pl.ds(zz * w2, w2), :], (((1,), (1,)), ((), ())),
                    preferred_element_type=F32,
                )
            place = zz - off // 2
            inside = is_root & (place >= 0) & (place < R // 2)
            part = part + jnp.where(inside, mir[jnp.clip(place, 0, R // 2 - 1)], 0.0)
            left, right = part[:, :w], part[:, w:]
            sends[d] = jnp.where(core == 0, right, left)
            s_sib(par, d).start()
            mine[d] = jnp.where(core == 0, left, right)
            if d + 2 < Z:
                pass_on(d + 2)
        pass_on(1)

        s_sib(par, 0).wait_recv()
        total = mine[0] + reds[par, 0]
        for d in range(1, R):
            s_col_in(par, row_of(d)).wait_recv()
            total = total + redc[par, row_of(d)].astype(F32)
        for d in range(1, Z):
            s_row_in(par, d).wait_recv()
            total = total + redr[par, chip(d)].astype(F32)

        first = k == 0
        scale = jnp.where(first, 1.0, 2.0)
        keep = jnp.where(first, 0.0, 1.0)
        current = out_ref[...]
        following = scale * (total - center_ref[0] * current) / half_ref[0] - keep * prev_ref[...]
        prev_ref[...] = current
        out_ref[...] = following
        for d in range(1, R):
            p_col(par, d).wait_send()
        for d in range(1, Z):
            p_row(par, d).wait_send()
        for d in range(Z):
            p_sib(par, d).wait_send()
        return carry

    lax.fori_loop(0, DEG, step, 0)
    wait_sums_sent((DEG - 1) % 2)


def body(R, C, start_block, center, half_width, matrix_tiles, tile_row, tile_col, tile_live):
    vectors, w = start_block.shape
    tile = matrix_tiles.shape[-1]
    own_clusters = w // tile
    ids = (tile_row[0], tile_col[0])
    sizes = (own_clusters * C, own_clusters * R)
    panel = build_panel(matrix_tiles[0], *ids, tile_live[0], *sizes)
    both = 2 * panel.size * 2 <= 24 * 2**20
    if both:
        flipped = build_panel(matrix_tiles[0], *ids[::-1], tile_live[0], *sizes[::-1], flip=True)
    else:
        flipped = jnp.zeros((16, 128), BF)
    vmem = pl.BlockSpec(memory_space=pltpu.VMEM)
    smem = pl.BlockSpec(memory_space=pltpu.SMEM)
    dma = pltpu.SemaphoreType.DMA
    flat = jax.ShapeDtypeStruct((vectors, w), F32)
    Z = C // 2
    panel_bytes = (panel.size + flipped.size) * 2
    return pl.pallas_call(
        functools.partial(filter_kernel, R, C, both),
        out_shape=(flat, flat),
        in_specs=[vmem, vmem, vmem, smem, smem],
        out_specs=(vmem, vmem),
        scratch_shapes=[
            pltpu.VMEM((2, C, vectors, w), BF),
            pltpu.VMEM((2, R, vectors, w), BF),
            pltpu.VMEM((Z, vectors, w), BF),
            pltpu.VMEM((R, vectors, w), BF),
            pltpu.VMEM((Z, vectors, w), F32),
            pltpu.VMEM((2, Z, vectors, w), BF),
            pltpu.VMEM((2, R, vectors, w), BF),
            pltpu.VMEM((2, Z, vectors, w), F32),
            pltpu.VMEM((R // 2, vectors, 2 * w), F32),
            pltpu.VMEM((Z, vectors, w), F32),
            dma((Z,)), dma((Z,)), dma((R,)), dma((2, C)), dma((2, R)),
            dma((Z,)), dma((Z,)), dma((R,)), dma((2, Z)), dma((2, Z)), dma((2, R)),
        ],
        compiler_params=pltpu.CompilerParams(
            collective_id=0, has_side_effects=True, vmem_limit_bytes=panel_bytes + 14 * 2**20
        ),
    )(panel, flipped, start_block, center, half_width)


def solution(mesh):
    R, C = mesh.shape["row"], mesh.shape["col"]
    in_specs = (
        P(None, ("row", "col")),
        P(),
        P(),
        P("row", "col", None, None),
        P("row", "col"),
        P("row", "col"),
        P("row", "col"),
    )
    out_specs = (P(None, ("row", "col")), P(None, ("row", "col")))
    return jax.shard_map(
        functools.partial(body, R, C), mesh=mesh, in_specs=in_specs, out_specs=out_specs, check_vma=False
    )
```

```python
import functools

import jax
import jax.numpy as jnp
from jax import lax
from jax.experimental import pallas as pl
from jax.experimental.pallas import tpu as pltpu
from jax.sharding import PartitionSpec as P

DEG = 8
MESH = pl.DeviceIdType.MESH
BF = jnp.bfloat16
F32 = jnp.float32


def build_kernel(slots, panel_cols, tile, flip, rows_ref, cols_ref, live_ref, tiles_ref, out_ref, head, link, acc):
    per_step = out_ref.shape[0] // tile
    step = pl.program_id(0)

    def load(s):
        block = tiles_ref[s]
        return (block.T if flip else block).astype(F32)

    @pl.when(step == 0)
    def _():
        @pl.loop(0, pl.num_programs(0) * per_step * panel_cols)
        def _(b):
            head[b] = -1

        @pl.loop(0, slots)
        def _(s):
            @pl.when(live_ref[s] > 0)
            def _():
                b = rows_ref[s] * panel_cols + cols_ref[s]
                link[s] = head[b]
                head[b] = s

    @pl.loop(0, per_step)
    def _(local):
        block_row = step * per_step + local
        rows = pl.ds(pl.multiple_of(local * tile, tile), tile)
        for pair in range(panel_cols // 2):
            here = [head[block_row * panel_cols + 2 * pair + side] for side in range(2)]
            empty = (here[0] < 0) & (here[1] < 0)
            columns = slice(pair * 2 * tile, (pair + 1) * 2 * tile)

            @pl.when(empty)
            def _(columns=columns):
                out_ref[rows, columns] = jnp.zeros((tile, 2 * tile), BF)

            @pl.when(jnp.logical_not(empty))
            def _(columns=columns, here=here):
                for side, s in enumerate(here):

                    @pl.when(s < 0)
                    def _(side=side):
                        acc[side] = jnp.zeros((tile, tile), F32)

                    @pl.when(s >= 0)
                    def _(side=side, s=s):
                        acc[side] = load(s)

                        def more(t):
                            acc[side] += load(t)
                            return link[t]

                        lax.while_loop(lambda t: t >= 0, more, link[s])

                both = jnp.concatenate([acc[0], acc[1]], axis=1)
                out_ref[rows, columns] = both.astype(BF)


def build_panel(tiles, row_ids, col_ids, live, panel_rows, panel_cols, flip=False):
    slots, tile, _ = tiles.shape
    per_step = 4
    smem = pl.BlockSpec(memory_space=pltpu.SMEM)
    return pl.pallas_call(
        functools.partial(build_kernel, slots, panel_cols, tile, flip),
        grid=(panel_rows // per_step,),
        out_shape=jax.ShapeDtypeStruct((panel_rows * tile, panel_cols * tile), BF),
        in_specs=[smem, smem, smem, pl.BlockSpec((slots, tile, tile), lambda i: (0, 0, 0))],
        out_specs=pl.BlockSpec((per_step * tile, panel_cols * tile), lambda i: (i, 0)),
        scratch_shapes=[
            pltpu.SMEM((panel_rows * panel_cols,), jnp.int32),
            pltpu.SMEM((slots,), jnp.int32),
            pltpu.VMEM((2, tile, tile), F32),
        ],
        compiler_params=pltpu.CompilerParams(vmem_limit_bytes=28 * 2**20),
    )(row_ids, col_ids, live, tiles)


def filter_kernel(
    R, C, both, panel_ref, flipped_ref, start_ref, center_ref, half_ref, out_ref, prev_ref,
    rowp, colp, sendr, sendc, sends, redr, redc, reds, mir, mine,
    ps_row, ps_sib, ps_col, pr_row, pr_col, rs_row, rs_sib, rs_col, rr_row, rr_sib, rr_col,
):
    w = start_ref.shape[1]
    w2 = 2 * w
    Z = C // 2
    r = lax.axis_index("row")
    c = lax.axis_index("col")
    z, core = c // 2, c % 2
    sib = c + 1 - 2 * core
    root_row = c * R // C
    off = c * R % C
    is_root = r == root_row
    not_root = r != root_row
    col_home = (r * C + c) // R
    col_slot = c % R

    def row_of(d):
        return (r + d) % R

    def chip(d):
        return 2 * ((z // 2 + d // 2) % (Z // 2)) + (z % 2 + d % 2) % 2

    def remote(src, dst, send_sem, recv_sem, row, col):
        return pltpu.make_async_remote_copy(
            src_ref=src, dst_ref=dst, send_sem=send_sem, recv_sem=recv_sem,
            device_id=(row, col), device_id_type=MESH,
        )

    barrier = pltpu.get_barrier_semaphore()
    pl.semaphore_signal(barrier, inc=1, device_id=(r, sib), device_id_type=MESH)
    for d in range(1, Z):
        pl.semaphore_signal(barrier, inc=1, device_id=(r, 2 * chip(d) + core), device_id_type=MESH)
    for d in range(1, R):
        pl.semaphore_signal(barrier, inc=1, device_id=(row_of(d), col_home), device_id_type=MESH)

    @pl.when(not_root)
    def _():
        for i in range(R):
            pl.semaphore_signal(barrier, inc=1, device_id=(root_row, off + i), device_id_type=MESH)

    pl.semaphore_wait(barrier, jnp.where(is_root, Z + R - 1, Z + 2 * R - 1))

    out_ref[...] = start_ref[...]
    prev_ref[...] = start_ref[...]

    def p_row(par, d):
        return remote(rowp.at[par, c], rowp.at[par, c], ps_row.at[d], pr_row.at[par, c], r, 2 * chip(d) + core)

    def p_in(par, src):
        return remote(rowp.at[par, src], rowp.at[par, src], ps_row.at[0], pr_row.at[par, src], r, src)

    def p_sib(par, d):
        src = 2 * chip(d) + core
        return remote(rowp.at[par, src], rowp.at[par, src], ps_sib.at[d], pr_row.at[par, src], r, sib)

    def p_col(par, d):
        return remote(rowp.at[par, c], colp.at[par, col_slot], ps_col.at[d], pr_col.at[par, col_slot], row_of(d), col_home)

    def p_col_in(par, i):
        return remote(colp.at[par, i], colp.at[par, i], ps_col.at[0], pr_col.at[par, i], root_row, off + i)

    def s_row(par, d):
        zz = chip(d)
        return remote(sendr.at[zz], redr.at[par, z], rs_row.at[d], rr_row.at[par, z], r, 2 * zz + core)

    def s_row_in(par, d):
        zz = chip(d)
        return remote(redr.at[par, zz], redr.at[par, zz], rs_row.at[0], rr_row.at[par, zz], r, 2 * zz + core)

    def s_sib(par, d):
        return remote(sends.at[d], reds.at[par, d], rs_sib.at[d], rr_sib.at[par, d], r, sib)

    def s_col(par, i):
        return remote(sendc.at[i], redc.at[par, r], rs_col.at[i], rr_col.at[par, r], root_row, off + i)

    def s_col_in(par, src):
        return remote(redc.at[par, src], redc.at[par, src], rs_col.at[0], rr_col.at[par, src], src, col_home)

    def wait_sums_sent(par):
        for d in range(1, Z):
            s_row(par, d).wait_send()
        for d in range(Z):
            s_sib(par, d).wait_send()

        @pl.when(not_root)
        def _():
            for i in range(R):
                s_col(par, i).wait_send()

    def step(k, carry):
        par = k % 2
        rowp[par, c] = out_ref[...].astype(BF)
        p_sib(par, 0).start()
        for d in range(Z - 1, 0, -1):
            p_row(par, d).start()
        for d in range(1, R):
            p_col(par, d).start()

        @pl.when(k > 0)
        def _():
            wait_sums_sent(1 - par)

        def arrive(d):
            p_in(par, 2 * chip(d) + core).wait_recv()
            p_sib(par, d).start()

        for d in range(Z):
            zz = chip(d)
            p_in(par, 2 * zz + 1 - core).wait_recv()
            lhs = jnp.concatenate([rowp[par, 2 * zz], rowp[par, 2 * zz + 1]], axis=1)
            part = jnp.dot(lhs, panel_ref[pl.ds(zz * w2, w2), :], preferred_element_type=F32)
            for i in range(R // 2):
                piece = part[:, i * w2 : (i + 1) * w2]
                if d == 0:
                    mir[i] = piece
                else:
                    mir[i] += piece
            if d == 0:
                arrive(1)
            if d + 2 < Z:
                arrive(d + 2)

        @pl.when(not_root)
        def _():
            for i in range(R):
                sendc[i] = mir[i // 2, :, (i % 2) * w : (i % 2 + 1) * w].astype(BF)
                s_col(par, i).start()
            for i in range(R):
                p_col_in(par, i).wait_recv()

        @pl.when(is_root)
        def _():
            for i in range(R):
                colp[par, i] = rowp[par, off + i]

        def pass_on(d):
            s_sib(par, d).wait_recv()
            sendr[chip(d)] = (mine[d] + reds[par, d]).astype(BF)
            s_row(par, d).start()

        x_col = jnp.concatenate([colp[par, i] for i in range(R)], axis=1)
        for d in range(Z - 1, -1, -1):
            zz = chip(d)
            if both:
                columns = pl.ds(pl.multiple_of(zz * w2, w2), w2)
                part = jnp.dot(x_col, flipped_ref[:, columns], preferred_element_type=F32)
            else:
                part = lax.dot_general(
                    x_col, panel_ref[pl.ds(zz * w2, w2), :], (((1,), (1,)), ((), ())),
                    preferred_element_type=F32,
                )
            place = zz - off // 2
            inside = is_root & (place >= 0) & (place < R // 2)
            part = part + jnp.where(inside, mir[jnp.clip(place, 0, R // 2 - 1)], 0.0)
            left, right = part[:, :w], part[:, w:]
            sends[d] = jnp.where(core == 0, right, left)
            s_sib(par, d).start()
            mine[d] = jnp.where(core == 0, left, right)
            if d + 2 < Z:
                pass_on(d + 2)
        pass_on(1)

        s_sib(par, 0).wait_recv()
        total = mine[0] + reds[par, 0]
        for d in range(1, R):
            s_col_in(par, row_of(d)).wait_recv()
            total = total + redc[par, row_of(d)].astype(F32)
        for d in range(1, Z):
            s_row_in(par, d).wait_recv()
            total = total + redr[par, chip(d)].astype(F32)

        first = k == 0
        scale = jnp.where(first, 1.0, 2.0)
        keep = jnp.where(first, 0.0, 1.0)
        current = out_ref[...]
        following = scale * (total - center_ref[0] * current) / half_ref[0] - keep * prev_ref[...]
        prev_ref[...] = current
        out_ref[...] = following
        for d in range(1, R):
            p_col(par, d).wait_send()
        for d in range(1, Z):
            p_row(par, d).wait_send()
        for d in range(Z):
            p_sib(par, d).wait_send()
        return carry

    lax.fori_loop(0, DEG, step, 0)
    wait_sums_sent((DEG - 1) % 2)


def body(R, C, start_block, center, half_width, matrix_tiles, tile_row, tile_col, tile_live):
    vectors, w = start_block.shape
    tile = matrix_tiles.shape[-1]
    own_clusters = w // tile
    ids = (tile_row[0], tile_col[0])
    sizes = (own_clusters * C, own_clusters * R)
    panel = build_panel(matrix_tiles[0], *ids, tile_live[0], *sizes)
    both = 2 * panel.size * 2 <= 24 * 2**20
    if both:
        flipped = build_panel(matrix_tiles[0], *ids[::-1], tile_live[0], *sizes[::-1], flip=True)
    else:
        flipped = jnp.zeros((16, 128), BF)
    vmem = pl.BlockSpec(memory_space=pltpu.VMEM)
    smem = pl.BlockSpec(memory_space=pltpu.SMEM)
    dma = pltpu.SemaphoreType.DMA
    flat = jax.ShapeDtypeStruct((vectors, w), F32)
    Z = C // 2
    panel_bytes = (panel.size + flipped.size) * 2
    return pl.pallas_call(
        functools.partial(filter_kernel, R, C, both),
        out_shape=(flat, flat),
        in_specs=[vmem, vmem, vmem, smem, smem],
        out_specs=(vmem, vmem),
        scratch_shapes=[
            pltpu.VMEM((2, C, vectors, w), BF),
            pltpu.VMEM((2, R, vectors, w), BF),
            pltpu.VMEM((Z, vectors, w), BF),
            pltpu.VMEM((R, vectors, w), BF),
            pltpu.VMEM((Z, vectors, w), F32),
            pltpu.VMEM((2, Z, vectors, w), BF),
            pltpu.VMEM((2, R, vectors, w), BF),
            pltpu.VMEM((2, Z, vectors, w), F32),
            pltpu.VMEM((R // 2, vectors, 2 * w), F32),
            pltpu.VMEM((Z, vectors, w), F32),
            dma((Z,)), dma((Z,)), dma((R,)), dma((2, C)), dma((2, R)),
            dma((Z,)), dma((Z,)), dma((R,)), dma((2, Z)), dma((2, Z)), dma((2, R)),
        ],
        compiler_params=pltpu.CompilerParams(
            collective_id=0, has_side_effects=True, vmem_limit_bytes=panel_bytes + 14 * 2**20
        ),
    )(panel, flipped, start_block, center, half_width)


def solution(mesh):
    R, C = mesh.shape["row"], mesh.shape["col"]
    in_specs = (
        P(None, ("row", "col")),
        P(),
        P(),
        P("row", "col", None, None),
        P("row", "col"),
        P("row", "col"),
        P("row", "col"),
    )
    out_specs = (P(None, ("row", "col")), P(None, ("row", "col")))
    return jax.shard_map(
        functools.partial(body, R, C), mesh=mesh, in_specs=in_specs, out_specs=out_specs, check_vma=False
    )
```
